32 devices in a mesh: obj: 4 (over x, core), mem: 8 (over z, y).
Axes of the slice: x: 2, y: 2, z: 4, core: 2. Of those that a mesh axis runs over, the one named last changes fastest.
Arguments:
- features: bfloat16 [2048, 512], P(('obj', 'mem')), may hold values from -6 to 6
- labels: int32 [2048], P('obj'), may hold values from 0 to 127
- block_weight: float32 [512, 512], replicated, may hold values from -0.25 to 0.25
- block_first: float32 [512, 512], replicated, may hold values from -3 to 3
- block_second: float32 [512, 512], replicated, may hold values from 0.04 to 0.16
- member_vectors: float32 [3, 8, 512], replicated, may hold values from -0.5 to 3.5, as said below
- vectors_first: float32 [3, 8, 512], replicated, may hold values from -0.625 to 0.625
- vectors_second: float32 [3, 8, 512], replicated, may hold values from 0.0016 to 0.0064
- head_weight: float32 [8, 512, 128], P('mem'), may hold values from -0.5 to 0.5
- head_first: float32 [8, 512, 128], P('mem'), may hold values from -0.75 to 0.75
- head_second: float32 [8, 512, 128], P('mem'), may hold values from 0.0025 to 0.01
- head_bias: float32 [8, 128], P('mem'), may hold values from -4 to 4
- bias_first: float32 [8, 128], P('mem'), may hold values from -1.25 to 1.25
- bias_second: float32 [8, 128], P('mem'), may hold values from 0.008 to 0.032
Outputs:
- mean_logits: float32 [2048, 128], P(('obj', 'mem'))
- features_grad: float32 [2048, 512], P(('obj', 'mem'))
- grad_norm: float32 [], replicated
- block_new: float32 [512, 512], replicated
- block_first_new: float32 [512, 512], replicated
- block_second_new: float32 [512, 512], replicated
- block_copy: bfloat16 [512, 512], replicated
- vectors_new: float32 [3, 8, 512], replicated
- vectors_first_new: float32 [3, 8, 512], replicated
- vectors_second_new: float32 [3, 8, 512], replicated
- head_new: float32 [8, 512, 128], P('mem')
- head_first_new: float32 [8, 512, 128], P('mem')
- head_second_new: float32 [8, 512, 128], P('mem')
- head_copy: bfloat16 [8, 512, 128], P('mem')
- bias_new: float32 [8, 128], P('mem')
- bias_first_new: float32 [8, 128], P('mem')
- bias_second_new: float32 [8, 128], P('mem')
The draws below stay inside these ranges and needn't reach their ends.
Inputs may be any that keep to these rules, and one draw needn't show every extreme that they name: `member_vectors`: entries of r and s are positive; b lies within -0.5 to 0.5.
All inputs are finite; a program needn't handle non-finite values.
Results may differ from the reference program's by a relative error of at most 0.012.
Values may be sent and summed in bfloat16 or wider, within the bound.
No kernel may reach another device: no remote copies, remote signals or barrier semaphores. Data moves between devices by JAX's collectives and lax.ppermute only.
A program may use at most 64 MiB of HBM per device.

```python
import math
import jax
import jax.numpy as jnp
from jax import lax

D = 512
C = 128
STEP = 5
MEMBERS = 8
OBJECTS = 2048


def draw_member_vectors(key, part):
    keys = jax.random.split(jax.random.fold_in(key, 11), 3)
    position = jnp.arange(MEMBERS, dtype=jnp.float32) / max(MEMBERS - 1, 1)
    scale_r = jnp.exp(jax.random.uniform(keys[0], (MEMBERS, D), jnp.float32, jnp.log(0.6), jnp.log(1.6)))
    rising = 0.6 * jnp.power(3.0, position)
    scale_s = rising[:, None] * jax.random.uniform(keys[1], (MEMBERS, D), jnp.float32, 0.7, 1.3)
    shift_b = jnp.clip(0.25 * jax.random.normal(keys[2], (MEMBERS, D), jnp.float32), -0.5, 0.5)
    return jnp.stack([scale_r, scale_s, shift_b]).astype(jnp.float32)


def with_ends(result, rng, least, high):
    spot = [jax.random.randint(jax.random.fold_in(rng, axis), (), 0, length) for axis, length in enumerate(result.shape)]
    widest = result.shape.index(max(result.shape))
    beside = spot[:widest] + [(spot[widest] + 1) % result.shape[widest]] + spot[widest + 1:]
    return result.at[tuple(spot)].set(least).at[tuple(beside)].set(high)


def steps_of(stream_key, extent, shards, smallest, high):
    loudness = 1.0
    for axis_at, parts in shards:
        heights = jax.random.uniform(jax.random.fold_in(jax.random.fold_in(stream_key, 6), axis_at), (parts,), jnp.float32, smallest / len(shards), high / len(shards))
        loudness = loudness * jnp.repeat(jnp.exp(heights), extent[axis_at] // parts).reshape((-1,) + (1,) * (len(extent) - 1 - axis_at))
    return loudness


def noise(stream_key, shape, width, most, cuts=(), kind=jnp.bfloat16):
    gain = steps_of(stream_key, shape, cuts, -0.22, 0.18) if cuts else 1.0
    entries = jax.random.normal(stream_key, shape, jnp.float32) * width * gain
    return jnp.minimum(jnp.maximum(entries, -most), most).astype(kind)


def setup_inputs(seed: int = 0) -> dict:
    streams_of = jax.random.split(jax.random.key(seed), 15)
    return {
        "features": noise(streams_of[0], (OBJECTS, D), 1.0, 6.0, ((0, 32),)),
        "labels": with_ends(jax.random.randint(streams_of[1], (OBJECTS,), 0, C), jax.random.fold_in(streams_of[1], 1), 0, C - 1).astype(jnp.int32),
        "block_weight": noise(streams_of[2], (D, D), D ** -0.5, 0.25, (), jnp.float32),
        "block_first": noise(streams_of[3], (D, D), 0.2, 3.0, (), jnp.float32),
        "block_second": jnp.clip(jnp.exp(jax.random.uniform(streams_of[4], (D, D), jnp.float32, math.log(0.04), math.log(0.16))), 0.04, 0.16),
        "member_vectors": draw_member_vectors(jax.random.fold_in(streams_of[14], 71), 0),
        "vectors_first": noise(streams_of[6], (3, MEMBERS, D), 0.04, 0.625, (), jnp.float32),
        "vectors_second": jnp.clip(jnp.exp(jax.random.uniform(streams_of[7], (3, MEMBERS, D), jnp.float32, math.log(0.0016), math.log(0.0064))), 0.0016, 0.0064),
        "head_weight": noise(streams_of[8], (MEMBERS, D, C), (D // 4) ** -0.5, 0.5, ((0, 8),), jnp.float32),
        "head_first": noise(streams_of[9], (MEMBERS, D, C), 0.05, 0.75, ((0, 8),), jnp.float32),
        "head_second": jnp.clip(jnp.exp(math.log(0.01) - 1.3862944 * jax.random.uniform(streams_of[10], (MEMBERS, D, C), jnp.float32) ** steps_of(streams_of[10], (MEMBERS, D, C), ((0, 8),), -0.2, 0.2)), 0.0025, 0.01),
        "head_bias": noise(streams_of[11], (MEMBERS, C), 0.3, 4.0, ((0, 8),), jnp.float32),
        "bias_first": noise(streams_of[12], (MEMBERS, C), 0.09, 1.25, ((0, 8),), jnp.float32),
        "bias_second": jnp.clip(jnp.exp(math.log(0.032) - 1.3862944 * jax.random.uniform(streams_of[13], (MEMBERS, C), jnp.float32) ** steps_of(streams_of[13], (MEMBERS, C), ((0, 8),), -0.2, 0.2)), 0.008, 0.032),
    }


@jax.custom_vjp
def low(v):
    return lax.optimization_barrier(v.astype(jnp.bfloat16)).astype(jnp.float32)

@jax.custom_vjp
def low_back(v):
    return v

def low_keep(v):
    return (low(v), None)

def low_pass(kept, grad):
    return (grad,)

def back_keep(v):
    return (v, None)

def back_low(kept, grad):
    return (low(grad),)
low.defvjp(low_keep, low_pass)
low_back.defvjp(back_keep, back_low)
clip_limit = 100.0
beta_one = 0.5
beta_two = 0.5
epsilon = 1e-08

def adamw(weight, grad, first, second, rate, decay):
    first_new = beta_one * first + (1.0 - beta_one) * grad
    second_new = beta_two * second + (1.0 - beta_two) * grad * grad
    fix_one = 1.0 - beta_one ** STEP
    fix_two = 1.0 - beta_two ** STEP
    step_size = first_new / fix_one / (jnp.sqrt(second_new / fix_two) + epsilon)
    return (weight - rate * (step_size + decay * weight), first_new, second_new)

def reference(features, labels, block_weight, block_first, block_second, member_vectors, vectors_first, vectors_second, head_weight, head_first, head_second, head_bias, bias_first, bias_second):
    highest = lax.Precision.HIGHEST
    onehot = (jnp.arange(C, dtype=jnp.int32)[None, None, :] == labels[:, None, None]).astype(jnp.float32)

    def forward(feat, weight, vectors, heads, biases):
        lifted = low(feat[:, None, :] * vectors[0][None])
        mixed = low_back(jnp.einsum('nmd,de->nme', lifted, low(weight), precision=highest))
        pre = mixed * vectors[1][None] + vectors[2][None]
        hidden = low(low_back(jax.nn.gelu(pre)))
        logits = low_back(jnp.einsum('nmd,mdc->nmc', hidden, low(heads), precision=highest)) + low(biases)[None]
        total = jax.nn.logsumexp(logits, axis=-1) - lax.optimization_barrier(jnp.sum(logits * onehot, axis=-1))
        return (jnp.sum(total), lax.optimization_barrier(jnp.mean(logits, axis=1)))
    feat = features.astype(jnp.float32)
    loss, back_fn, mean_logits = jax.vjp(forward, feat, block_weight, member_vectors, head_weight, head_bias, has_aux=True)
    feat_grad, block_grad, vectors_grad, head_grad, bias_grad = back_fn(jnp.ones_like(loss))
    squares = jnp.sum(block_grad * block_grad) + jnp.sum(vectors_grad * vectors_grad) + jnp.sum(head_grad * head_grad) + jnp.sum(bias_grad * bias_grad)
    grad_norm = jnp.sqrt(squares)
    factor = clip_limit / jnp.maximum(grad_norm, clip_limit)
    block_new, block_m, block_v = adamw(block_weight, block_grad * factor, block_first, block_second, 0.02, 0.01)
    vectors_new, vectors_m, vectors_v = adamw(member_vectors, vectors_grad * factor, vectors_first, vectors_second, 0.5, 0.0)
    head_new, head_m, head_v = adamw(head_weight, head_grad * factor, head_first, head_second, 0.02, 0.01)
    bias_new, bias_m, bias_v = adamw(head_bias, bias_grad * factor, bias_first, bias_second, 0.1, 0.0)
    return (mean_logits, feat_grad, grad_norm, block_new, block_m, block_v, block_new.astype(jnp.bfloat16), vectors_new, vectors_m, vectors_v, head_new, head_m, head_v, head_new.astype(jnp.bfloat16), bias_new, bias_m, bias_v)
```

```python
import functools
import math

import jax
import jax.numpy as jnp
from jax import lax
from jax.experimental import pallas as pl
from jax.experimental.pallas import tpu as pltpu
from jax.sharding import PartitionSpec as P

STEP = 5
ALL = ("obj", "mem")
LANES = 128
PAD = 16
MIB = 1 << 20

clip_limit = 100.0
beta_one = 0.5
beta_two = 0.5
epsilon = 1e-08
gelu_in = math.sqrt(2.0 / math.pi)
gelu_cube = 0.044715

bf16 = jnp.bfloat16
f32 = jnp.float32
VMEM = pl.BlockSpec(memory_space=pltpu.VMEM)
SMEM = pl.BlockSpec(memory_space=pltpu.SMEM)


def adamw(weight, grad, first, second, rate, decay):
    first_new = beta_one * first + (1.0 - beta_one) * grad
    second_new = beta_two * second + (1.0 - beta_two) * grad * grad
    fix_one = 1.0 - beta_one**STEP
    fix_two = 1.0 - beta_two**STEP
    step_size = first_new / fix_one / (jnp.sqrt(second_new / fix_two) + epsilon)
    return (weight - rate * (step_size + decay * weight), first_new, second_new)


def dot(a, b, dims=((1,), (0,))):
    return lax.dot_general(a, b, (dims, ((), ())), preferred_element_type=f32)


def call(body, outs, args, scratch=(), name=None):
    specs = [SMEM] + [VMEM] * (len(args) - 1)
    return pl.pallas_call(
        body,
        out_shape=outs,
        in_specs=specs,
        out_specs=jax.tree.map(lambda _: VMEM, outs),
        scratch_shapes=list(scratch),
        compiler_params=pltpu.CompilerParams(vmem_limit_bytes=40 * MIB),
        name=name,
    )(*args)


class Plan:
    def __init__(self, mesh, width, classes, rows):
        self.n_obj, self.n_mem = mesh.shape["obj"], mesh.shape["mem"]
        self.outer = self.n_mem // 2
        self.quads = self.n_obj
        self.shards = 2 * self.quads
        self.width, self.classes, self.rows = width, classes, rows
        self.groups = width // LANES
        self.block_rows = width // self.shards
        self.stacked = self.block_rows * self.groups
        self.items = max(8, self.shards)

    def perm(self, move):
        pairs = []
        for obj in range(self.n_obj):
            for mem in range(self.n_mem):
                to_obj, to_mem = move(obj, mem)
                pairs.append((obj * self.n_mem + mem, to_obj * self.n_mem + to_mem))
        return pairs

    def over_core(self, v):
        return lax.ppermute(v, ALL, self.perm(lambda o, m: (o ^ 1, m)))

    def over_plane(self, v, k):
        return lax.ppermute(v, ALL, self.perm(lambda o, m: (o ^ (k >> 1 << 1), m ^ (k & 1))))

    def over_outer(self, v, k):
        return lax.ppermute(v, ALL, self.perm(lambda o, m: (o, m ^ (k << 1))))


def local_body(plan, place, *refs):
    n = plan.outer
    feats = refs[:n]
    onehot_ref, weight_ref, vec_ref, own_head, own_bias, far_head = refs[n : n + 6]
    send_ref, keep_ref = refs[n + 6 : n + 8]
    back_own = refs[n + 8]
    back_far = refs[n + 9 : n + 8 + n]
    lifted_ref, mixed_ref, hidden_ref, slope_ref, dmixed_ref, block_ref, heads_ref, items_ref = refs[
        n + 8 + n :
    ]
    rows, width, classes = plan.rows, plan.width, plan.classes
    objs = n * rows
    core, quad, outer, inner = place[0], place[1], place[2], place[3]
    tile = 16

    for j in range(2):
        scale_r = vec_ref[j : j + 1, :]
        for k in range(n):
            lifted_ref[j * objs + k * rows : j * objs + (k + 1) * rows, :] = (
                feats[k][...].astype(f32) * scale_r
            ).astype(bf16)
    mixed_ref[...] = dot(lifted_ref[...], weight_ref[...])

    items_ref[...] = jnp.zeros_like(items_ref)
    for j in range(2):
        scale_s = vec_ref[2 + j : 3 + j, :]
        shift_b = vec_ref[4 + j : 5 + j, :]

        def forward(t, carry):
            at = pl.ds(pl.multiple_of(j * objs + t * tile, tile), tile)
            pre = mixed_ref[at, :] * scale_s + shift_b
            square = pre * pre
            bend = jnp.tanh(gelu_in * (pre + gelu_cube * square * pre))
            hidden_ref[at, :] = (0.5 * pre * (1.0 + bend)).astype(bf16)
            slope_ref[at, :] = 0.5 * (1.0 + bend) + (0.5 * gelu_in) * pre * (1.0 - bend * bend) * (
                1.0 + (3.0 * gelu_cube) * square
            )
            return carry

        lax.fori_loop(0, objs // tile, forward, 0, unroll=2)

    logit_sum = None
    for j in range(2):
        mine = inner == j
        head = jnp.where(mine, own_head[...], far_head[0:width, :])
        bias = jnp.where(mine, own_bias[0:1, :], far_head[width : width + 1, :]).astype(f32)
        hidden = hidden_ref[j * objs : (j + 1) * objs, :]
        logits = dot(hidden, head) + bias
        logit_sum = logits if logit_sum is None else logit_sum + logits
        top = jnp.max(logits, axis=-1, keepdims=True)
        grown = jnp.exp(logits - top)
        soft = grown / jnp.sum(grown, axis=-1, keepdims=True)
        hot = jnp.concatenate(
            [
                onehot_ref[pl.ds(pl.multiple_of(((outer ^ k) * 2 + inner) * rows, rows), rows), :]
                for k in range(n)
            ],
            axis=0,
        )
        dlogits = soft - hot
        dlow = dlogits.astype(bf16)
        items_ref[6 + j, 0:1, :] = jnp.sum(dlogits, axis=0, keepdims=True)
        heads_ref[j] = dot(hidden, dlow, ((0,), (0,)))
        mixed_back = dot(dlow, head, ((1,), (1,)))
        block_ref[0:objs, :] = mixed_back
        scale_s = vec_ref[2 + j : 3 + j, :]

        def backward(t, carry):
            s_sum, b_sum = carry
            at = pl.ds(pl.multiple_of(j * objs + t * tile, tile), tile)
            near = pl.ds(pl.multiple_of(t * tile, tile), tile)
            dpre = block_ref[near, :].astype(bf16).astype(f32) * slope_ref[at, :]
            dmixed_ref[at, :] = (dpre * scale_s).astype(bf16)
            return s_sum + dpre * mixed_ref[at, :], b_sum + dpre

        zero = jnp.zeros((tile, width), f32)
        s_sum, b_sum = lax.fori_loop(0, objs // tile, backward, (zero, zero), unroll=2)
        s_grad = jnp.sum(s_sum, axis=0, keepdims=True)
        b_grad = jnp.sum(b_sum, axis=0, keepdims=True)
        for g in range(plan.groups):
            at = slice(g * LANES, (g + 1) * LANES)
            items_ref[2 + j, g : g + 1, :] = s_grad[:, at]
            items_ref[4 + j, g : g + 1, :] = b_grad[:, at]

    block_ref[0:width, :] = dot(lifted_ref[...], dmixed_ref[...], ((0,), (0,)))
    slope_ref[...] = dot(dmixed_ref[...], weight_ref[...], ((1,), (1,)))
    r_sums = [jnp.zeros((1, width), f32) for _ in range(2)]
    for k in range(n):
        feat = feats[k][...].astype(f32)
        back = None
        for j in range(2):
            lift_back = slope_ref[j * objs + k * rows : j * objs + (k + 1) * rows, :]
            r_sums[j] = r_sums[j] + jnp.sum(lift_back * feat, axis=0, keepdims=True)
            part = lift_back * vec_ref[j : j + 1, :]
            back = part if back is None else back + part
        out = back_own if k == 0 else back_far[k - 1]
        out[:, 0:width] = back.astype(out.dtype)
        out[:, width : width + classes] = logit_sum[k * rows : (k + 1) * rows, :].astype(out.dtype)
    for j in range(2):
        for g in range(plan.groups):
            items_ref[j, g : g + 1, :] = r_sums[j][:, g * LANES : (g + 1) * LANES]

    stride = plan.block_rows
    for out, side in ((keep_ref, core), (send_ref, 1 - core)):
        for k in range(plan.quads):
            shard = side * plan.quads + (quad ^ k)
            at = pl.ds(pl.multiple_of(shard * stride, stride), stride)
            for g in range(plan.groups):
                out[k, g * stride : (g + 1) * stride, :] = block_ref[
                    at, g * LANES : (g + 1) * LANES
                ].astype(out.dtype)
            base = plan.stacked
            for j in range(2):
                out[k, base : base + stride, :] = heads_ref[j, at, :].astype(out.dtype)
                base += stride
            out[k, base : base + PAD, :] = items_ref[shard].astype(out.dtype)


def core_body(plan, place, keep_ref, got_ref, own_ref, *send_refs):
    own_ref[...] = keep_ref[0] + got_ref[0].astype(f32)
    for k in range(1, plan.quads):
        send_refs[k - 1][...] = (keep_ref[k] + got_ref[k].astype(f32)).astype(bf16)


def two_parts(v):
    high = v.astype(bf16).astype(f32)
    return high, v - high


def plane_body(plan, place, own_ref, *refs):
    got, (send_ref, block_ref, head_ref) = refs[: plan.quads - 1], refs[plan.quads - 1 :]
    total = own_ref[...]
    for r in got:
        total = total + r[...].astype(f32)
    base = plan.stacked
    block_ref[0:base, :] = total[0:base, :]
    send_ref[0:base, :] = total[0:base, :].astype(bf16)
    heads = total[base : base + 2 * plan.block_rows, :]
    head_ref[...] = heads
    squares = jnp.sum(jnp.sum(heads * heads, axis=1, keepdims=True), axis=0, keepdims=True)
    high, low = two_parts(jnp.broadcast_to(squares, (PAD, LANES)))
    items = total[base + 2 * plan.block_rows :, :]
    row = lax.broadcasted_iota(jnp.int32, (PAD, LANES), 0)
    extra = jnp.where(row < plan.groups, items, jnp.where(row == plan.groups, high, low))
    block_ref[base : base + PAD, :] = extra
    send_ref[base : base + PAD, :] = extra.astype(bf16)


def outer_body(plan, place, block_ref, head_ref, *refs):
    n = plan.outer
    got, (same_ref, flip_ref) = refs[: n - 1], refs[n - 1 :]
    inner = place[3]
    base, stride, groups = plan.stacked, plan.block_rows, plan.groups
    total = block_ref[0:base, :]
    extras = [block_ref[base : base + PAD, :].astype(bf16).astype(f32)]
    for r in got:
        total = total + r[0:base, :].astype(f32)
        extras.append(r[base : base + PAD, :].astype(f32))
    row = lax.broadcasted_iota(jnp.int32, (PAD, LANES), 0)
    head_squares = jnp.zeros((1, LANES), f32)
    item_squares = jnp.zeros((PAD, LANES), f32)
    for extra in extras:
        head_squares = head_squares + extra[groups : groups + 1, :] + extra[groups + 1 : groups + 2, :]
        item_squares = item_squares + jnp.where(row < groups, extra * extra, 0.0)
    squares = (
        jnp.sum(jnp.sum(total * total, axis=1, keepdims=True), axis=0, keepdims=True)
        + jnp.sum(jnp.sum(item_squares, axis=1, keepdims=True), axis=0, keepdims=True)
        + head_squares
    )
    high, low = two_parts(jnp.broadcast_to(squares, (PAD, LANES)))
    items = jnp.concatenate([extra[0:groups, :] for extra in extras], axis=0).astype(bf16)
    sums = jnp.where(row == 0, high, low).astype(bf16)
    block = total.astype(bf16)
    for out, member in ((same_ref, inner), (flip_ref, 1 - inner)):
        at = pl.ds(pl.multiple_of(member * stride, stride), stride)
        out[0:base, :] = block
        out[base : base + groups * n, :] = items
        spot = base + groups * n
        out[spot : spot + stride, :] = head_ref[at, :].astype(bf16)
        out[spot + stride : spot + stride + PAD, :] = sums


def back_body(plan, place, own_ref, *refs):
    got, (feat_ref, mean_ref) = refs[: plan.outer - 1], refs[plan.outer - 1 :]
    total = own_ref[...]
    for r in got:
        total = total + r[...].astype(f32)
    feat_ref[...] = total[:, 0 : plan.width]
    mean_ref[...] = total[:, plan.width :] / plan.n_mem


def update_body(plan, place, *refs):
    chunks = refs[: plan.shards]
    (bw, bm, bv, vw, vm, vv, hw, hm, hv, cw, cm, cv) = refs[plan.shards : plan.shards + 12]
    (
        norm_ref,
        bw_out,
        bm_out,
        bv_out,
        bcopy_out,
        vw_out,
        vm_out,
        vv_out,
        hw_out,
        hm_out,
        hv_out,
        hcopy_out,
        cw_out,
        cm_out,
        cv_out,
        items_ref,
    ) = refs[plan.shards + 12 :]
    core, quad, outer, inner = place[0], place[1], place[2], place[3]
    n, groups, stride, base = plan.outer, plan.groups, plan.block_rows, plan.stacked
    spot = base + groups * n
    squares = jnp.zeros((1, LANES), f32)
    for chunk in chunks:
        sums = chunk[spot + stride : spot + stride + PAD, :].astype(f32)
        squares = squares + sums[0:1, :] + sums[1:2, :]
    norm = jnp.sqrt(squares)
    norm_ref[...] = norm
    factor = clip_limit / jnp.maximum(norm, clip_limit)

    for i, chunk in enumerate(chunks):
        side, k = divmod(i, plan.quads)
        shard = (core ^ side) * plan.quads + (quad ^ k)
        at = pl.ds(pl.multiple_of(shard * stride, stride), stride)
        for g in range(groups):
            lanes = slice(g * LANES, (g + 1) * LANES)
            grad = chunk[g * stride : (g + 1) * stride, :].astype(f32) * factor
            w, m, v = adamw(bw[at, lanes], grad, bm[at, lanes], bv[at, lanes], 0.02, 0.01)
            bw_out[at, lanes] = w
            bm_out[at, lanes] = m
            bv_out[at, lanes] = v
            bcopy_out[at, lanes] = w.astype(bf16)
        grad = chunk[spot : spot + stride, :].astype(f32) * factor
        w, m, v = adamw(hw[at, :], grad, hm[at, :], hv[at, :], 0.02, 0.01)
        hw_out[at, :] = w
        hm_out[at, :] = m
        hv_out[at, :] = v
        hcopy_out[at, :] = w.astype(bf16)
        items = chunk[base : base + groups * n, :].astype(f32)
        kind, member = shard // 2, shard % 2
        for z in range(n):
            items_ref[kind, (outer ^ z) * 2 + member] = items[z * groups : (z + 1) * groups, :]

    wide = jnp.concatenate([factor] * groups, axis=1)
    for t in range(3):
        grad = jnp.concatenate([items_ref[t, :, g, :] for g in range(groups)], axis=1) * wide
        w, m, v = adamw(vw[t], grad, vm[t], vv[t], 0.5, 0.0)
        vw_out[t] = w
        vm_out[t] = m
        vv_out[t] = v
    grad = items_ref[3, outer * 2 + inner, 0:1, :] * factor
    w, m, v = adamw(cw[...], grad, cm[...], cv[...], 0.1, 0.0)
    cw_out[...] = w
    cm_out[...] = m
    cv_out[...] = v


def on_device(
    mesh,
    features,
    labels,
    block_weight,
    block_first,
    block_second,
    member_vectors,
    vectors_first,
    vectors_second,
    head_weight,
    head_first,
    head_second,
    head_bias,
    bias_first,
    bias_second,
):
    rows, width = features.shape
    classes = head_weight.shape[-1]
    plan = Plan(mesh, width, classes, rows)
    n, quads, stride = plan.outer, plan.quads, plan.block_rows
    shape = jax.ShapeDtypeStruct
    obj, mem = lax.axis_index("obj"), lax.axis_index("mem")
    outer, inner = mem // 2, mem % 2
    place = jnp.stack([obj % 2, obj // 2 * 2 + inner, outer, inner]).astype(jnp.int32)

    far_feats = [plan.over_outer(features, k) for k in range(1, n)]
    head_low = head_weight[0].astype(bf16)
    bias_low = jnp.broadcast_to(head_bias.astype(bf16), (PAD, classes))
    far_head = plan.over_plane(jnp.concatenate([head_low, bias_low], axis=0), 1)
    onehot = (
        jnp.arange(classes, dtype=jnp.int32)[None, :] == labels[:, None]
    ).astype(f32)
    weight_low = block_weight.astype(bf16)
    pair = lax.dynamic_slice_in_dim(member_vectors, outer * 2, 2, axis=1).reshape(6, width)

    objs = n * rows
    total = plan.stacked + 2 * stride + PAD
    back = width + classes
    outs = call(
        functools.partial(local_body, plan),
        [
            shape((quads, total, LANES), bf16),
            shape((quads, total, LANES), f32),
            shape((rows, back), f32),
        ]
        + [shape((rows, back), bf16)] * (n - 1),
        [place, features, *far_feats, onehot, weight_low, pair, head_low, bias_low, far_head],
        [
            pltpu.VMEM((2 * objs, width), bf16),
            pltpu.VMEM((2 * objs, width), f32),
            pltpu.VMEM((2 * objs, width), bf16),
            pltpu.VMEM((2 * objs, width), f32),
            pltpu.VMEM((2 * objs, width), bf16),
            pltpu.VMEM((max(width, objs), width), f32),
            pltpu.VMEM((2, width, classes), f32),
            pltpu.VMEM((plan.items, PAD, LANES), f32),
        ],
        name="local",
    )
    send, keep, back_own, back_far = outs[0], outs[1], outs[2], outs[3:]

    got = plan.over_core(send)
    own, *sends = call(
        functools.partial(core_body, plan),
        [shape((total, LANES), f32)] + [shape((total, LANES), bf16)] * (quads - 1),
        [place, keep, got],
        name="core_sum",
    )
    got = [plan.over_plane(v, k + 1) for k, v in enumerate(sends)]
    send, block, heads = call(
        functools.partial(plane_body, plan),
        [
            shape((plan.stacked + PAD, LANES), bf16),
            shape((plan.stacked + PAD, LANES), f32),
            shape((2 * stride, LANES), f32),
        ],
        [place, own, *got],
        name="plane_sum",
    )
    got = [plan.over_outer(send, k) for k in range(1, n)]
    last = plan.stacked + plan.groups * n + stride + PAD
    same, flip = call(
        functools.partial(outer_body, plan),
        [shape((last, LANES), bf16)] * 2,
        [place, block, heads, *got],
        name="outer_sum",
    )
    near = [same] + [plan.over_plane(flip if k & 1 else same, k) for k in range(1, quads)]
    far = [plan.over_core(v) for v in near]

    back_got = [plan.over_outer(v, k + 1) for k, v in enumerate(back_far)]
    features_grad, mean_logits = call(
        functools.partial(back_body, plan),
        [shape((rows, width), f32), shape((rows, classes), f32)],
        [place, back_own, *back_got],
        name="back_sum",
    )

    like = lambda v, dtype=f32: shape(v.shape, dtype)
    head_w, head_m, head_v = head_weight[0], head_first[0], head_second[0]
    (norm, bw, bm, bv, bcopy, vw, vm, vv, hw, hm, hv, hcopy, cw, cm, cv) = call(
        functools.partial(update_body, plan),
        [shape((1, LANES), f32)]
        + [like(block_weight)] * 3
        + [like(block_weight, bf16)]
        + [like(member_vectors)] * 3
        + [like(head_w)] * 3
        + [like(head_w, bf16)]
        + [like(head_bias)] * 3,
        [
            place,
            *near,
            *far,
            block_weight,
            block_first,
            block_second,
            member_vectors,
            vectors_first,
            vectors_second,
            head_w,
            head_m,
            head_v,
            head_bias,
            bias_first,
            bias_second,
        ],
        [pltpu.VMEM((plan.items // 2, plan.n_mem, plan.groups, LANES), f32)],
        name="update",
    )
    return (
        mean_logits,
        features_grad,
        norm[0, 0],
        bw,
        bm,
        bv,
        bcopy,
        vw,
        vm,
        vv,
        hw[None],
        hm[None],
        hv[None],
        hcopy[None],
        cw,
        cm,
        cv,
    )


def solution(mesh):
    split, whole = P(ALL, None), P()
    heads, biases = P("mem", None, None), P("mem", None)
    return jax.shard_map(
        functools.partial(on_device, mesh),
        mesh=mesh,
        in_specs=(split, P("obj")) + (whole,) * 6 + (heads,) * 3 + (biases,) * 3,
        out_specs=(split, split) + (whole,) * 8 + (heads,) * 4 + (biases,) * 3,
        check_vma=False,
    )
```

```python
import functools
import math

import jax
import jax.numpy as jnp
from jax import lax
from jax.experimental import pallas as pl
from jax.experimental.pallas import tpu as pltpu
from jax.sharding import PartitionSpec as P

STEP = 5
ALL = ("obj", "mem")
LANES = 128
PAD = 16
MIB = 1 << 20

clip_limit = 100.0
beta_one = 0.5
beta_two = 0.5
epsilon = 1e-08
gelu_in = math.sqrt(2.0 / math.pi)
gelu_cube = 0.044715

bf16 = jnp.bfloat16
f32 = jnp.float32
VMEM = pl.BlockSpec(memory_space=pltpu.VMEM)
SMEM = pl.BlockSpec(memory_space=pltpu.SMEM)


def adamw(weight, grad, first, second, rate, decay):
    first_new = beta_one * first + (1.0 - beta_one) * grad
    second_new = beta_two * second + (1.0 - beta_two) * grad * grad
    fix_one = 1.0 - beta_one**STEP
    fix_two = 1.0 - beta_two**STEP
    step_size = first_new / fix_one / (jnp.sqrt(second_new / fix_two) + epsilon)
    return (weight - rate * (step_size + decay * weight), first_new, second_new)


def dot(a, b, dims=((1,), (0,))):
    return lax.dot_general(a, b, (dims, ((), ())), preferred_element_type=f32)


def call(body, outs, args, scratch=(), name=None, out_spec=VMEM):
    specs = [VMEM] * len(args)
    return pl.pallas_call(
        body,
        out_shape=outs,
        in_specs=specs,
        out_specs=[out_spec] * len(outs),
        scratch_shapes=list(scratch),
        compiler_params=pltpu.CompilerParams(vmem_limit_bytes=40 * MIB),
        name=name,
    )(*args)


class Plan:
    def __init__(self, mesh, width, classes, rows):
        self.n_obj, self.n_mem = mesh.shape["obj"], mesh.shape["mem"]
        self.outer = self.n_mem // 2
        self.quads = self.n_obj
        self.shards = 2 * self.quads
        self.width, self.classes, self.rows = width, classes, rows
        self.groups = width // LANES
        self.block_rows = width // self.shards
        self.stacked = self.block_rows * self.groups
        self.items = max(8, self.shards)
        self.bits = [1 << i for i in range(self.outer.bit_length() - 1)]
        self.halving = sorted(range(self.outer), key=lambda k: [k & bit for bit in self.bits])

    def perm(self, move):
        pairs = []
        for obj in range(self.n_obj):
            for mem in range(self.n_mem):
                to_obj, to_mem = move(obj, mem)
                pairs.append((obj * self.n_mem + mem, to_obj * self.n_mem + to_mem))
        return pairs

    def over_core(self, v):
        return lax.ppermute(v, ALL, self.perm(lambda o, m: (o ^ 1, m)))

    def over_plane(self, v, k):
        return lax.ppermute(v, ALL, self.perm(lambda o, m: (o ^ (k >> 1 << 1), m ^ (k & 1))))

    def over_outer(self, v, k):
        return lax.ppermute(v, ALL, self.perm(lambda o, m: (o, m ^ (k << 1))))


def local_body(plan, *refs):
    n = plan.outer
    feats = refs[:n]
    onehot_ref, weight_ref, vec_ref, own_head, own_bias, far_head = refs[n : n + 6]
    send_ref, keep_ref = refs[n + 6 : n + 8]
    back_keep, back_send = refs[n + 8 : n + 10]
    lifted_ref, mixed_ref, hidden_ref, slope_ref, dmixed_ref, block_ref, heads_ref, items_ref = refs[
        n + 10 :
    ]
    rows, width, classes = plan.rows, plan.width, plan.classes
    objs = n * rows
    core, quad, outer, inner = place_of()
    tile = 16

    for j in range(2):
        scale_r = vec_ref[j : j + 1, :]
        for k in range(n):
            lifted_ref[j * objs + k * rows : j * objs + (k + 1) * rows, :] = (
                feats[k][...].astype(f32) * scale_r
            ).astype(bf16)
    mixed_ref[...] = dot(lifted_ref[...], weight_ref[...])

    items_ref[...] = jnp.zeros_like(items_ref)
    for j in range(2):
        scale_s = vec_ref[2 + j : 3 + j, :]
        shift_b = vec_ref[4 + j : 5 + j, :]

        def forward(t, carry):
            at = pl.ds(pl.multiple_of(j * objs + t * tile, tile), tile)
            pre = mixed_ref[at, :] * scale_s + shift_b
            square = pre * pre
            bend = jnp.tanh(gelu_in * (pre + gelu_cube * square * pre))
            hidden_ref[at, :] = (0.5 * pre * (1.0 + bend)).astype(bf16)
            slope_ref[at, :] = 0.5 * (1.0 + bend) + (0.5 * gelu_in) * pre * (1.0 - bend * bend) * (
                1.0 + (3.0 * gelu_cube) * square
            )
            return carry

        lax.fori_loop(0, objs // tile, forward, 0, unroll=2)

    logit_sum = None
    for j in range(2):
        mine = inner == j
        head = jnp.where(mine, own_head[...], far_head[0:width, :])
        bias = jnp.where(mine, own_bias[0:1, :], far_head[width : width + 1, :]).astype(f32)
        hidden = hidden_ref[j * objs : (j + 1) * objs, :]
        logits = dot(hidden, head) + bias
        logit_sum = logits if logit_sum is None else logit_sum + logits
        top = jnp.max(logits, axis=-1, keepdims=True)
        grown = jnp.exp(logits - top)
        soft = grown / jnp.sum(grown, axis=-1, keepdims=True)
        hot = jnp.concatenate(
            [
                onehot_ref[pl.ds(pl.multiple_of(((outer ^ k) * 2 + inner) * rows, rows), rows), :]
                for k in range(n)
            ],
            axis=0,
        )
        dlogits = soft - hot
        dlow = dlogits.astype(bf16)
        items_ref[6 + j, 0:1, :] = jnp.sum(dlogits, axis=0, keepdims=True)
        heads_ref[j] = dot(hidden, dlow, ((0,), (0,)))
        mixed_back = dot(dlow, head, ((1,), (1,)))
        block_ref[0:objs, :] = mixed_back
        scale_s = vec_ref[2 + j : 3 + j, :]

        def backward(t, carry):
            s_sum, b_sum = carry
            at = pl.ds(pl.multiple_of(j * objs + t * tile, tile), tile)
            near = pl.ds(pl.multiple_of(t * tile, tile), tile)
            dpre = block_ref[near, :].astype(bf16).astype(f32) * slope_ref[at, :]
            dmixed_ref[at, :] = (dpre * scale_s).astype(bf16)
            return s_sum + dpre * mixed_ref[at, :], b_sum + dpre

        zero = jnp.zeros((tile, width), f32)
        s_sum, b_sum = lax.fori_loop(0, objs // tile, backward, (zero, zero), unroll=2)
        s_grad = jnp.sum(s_sum, axis=0, keepdims=True)
        b_grad = jnp.sum(b_sum, axis=0, keepdims=True)
        for g in range(plan.groups):
            at = slice(g * LANES, (g + 1) * LANES)
            items_ref[2 + j, g : g + 1, :] = s_grad[:, at]
            items_ref[4 + j, g : g + 1, :] = b_grad[:, at]

    block_ref[0:width, :] = dot(lifted_ref[...], dmixed_ref[...], ((0,), (0,)))
    slope_ref[...] = dot(dmixed_ref[...], weight_ref[...], ((1,), (1,)))
    r_sums = [jnp.zeros((1, width), f32) for _ in range(2)]
    for spot, k in enumerate(plan.halving):
        feat = feats[k][...].astype(f32)
        back = None
        for j in range(2):
            lift_back = slope_ref[j * objs + k * rows : j * objs + (k + 1) * rows, :]
            r_sums[j] = r_sums[j] + jnp.sum(lift_back * feat, axis=0, keepdims=True)
            part = lift_back * vec_ref[j : j + 1, :]
            back = part if back is None else back + part
        out = back_keep if spot < n // 2 else back_send
        at = slice(spot % (n // 2) * rows, (spot % (n // 2) + 1) * rows)
        out[at, 0:width] = back.astype(out.dtype)
        out[at, width : width + classes] = logit_sum[k * rows : (k + 1) * rows, :].astype(out.dtype)
    for j in range(2):
        for g in range(plan.groups):
            items_ref[j, g : g + 1, :] = r_sums[j][:, g * LANES : (g + 1) * LANES]

    stride = plan.block_rows
    for out, side in ((keep_ref, core), (send_ref, 1 - core)):
        for k in range(plan.quads):
            shard = side * plan.quads + (quad ^ k)
            at = pl.ds(pl.multiple_of(shard * stride, stride), stride)
            for g in range(plan.groups):
                out[k, g * stride : (g + 1) * stride, :] = block_ref[
                    at, g * LANES : (g + 1) * LANES
                ].astype(out.dtype)
            base = plan.stacked
            for j in range(2):
                out[k, base : base + stride, :] = heads_ref[j, at, :].astype(out.dtype)
                base += stride
            out[k, base : base + PAD, :] = items_ref[shard].astype(out.dtype)


def core_body(plan, keep_ref, got_ref, own_ref, *send_refs):
    own_ref[...] = keep_ref[0] + got_ref[0].astype(f32)
    for k in range(1, plan.quads):
        send_refs[k - 1][...] = (keep_ref[k] + got_ref[k].astype(f32)).astype(bf16)


def place_of():
    obj, mem = lax.axis_index("obj"), lax.axis_index("mem")
    return obj % 2, obj // 2 * 2 + mem % 2, mem // 2, mem % 2


def two_parts(v):
    high = v.astype(bf16).astype(f32)
    return high, v - high


def plane_body(plan, own_ref, *refs):
    got, (send_ref, block_ref, head_ref) = refs[: plan.quads - 1], refs[plan.quads - 1 :]
    total = own_ref[...]
    for r in got:
        total = total + r[...].astype(f32)
    base = plan.stacked
    block_ref[0:base, :] = total[0:base, :]
    send_ref[0:base, :] = total[0:base, :].astype(bf16)
    heads = total[base : base + 2 * plan.block_rows, :]
    head_ref[...] = heads
    squares = jnp.sum(jnp.sum(heads * heads, axis=1, keepdims=True), axis=0, keepdims=True)
    high, low = two_parts(jnp.broadcast_to(squares, (PAD, LANES)))
    items = total[base + 2 * plan.block_rows :, :]
    row = lax.broadcasted_iota(jnp.int32, (PAD, LANES), 0)
    extra = jnp.where(row < plan.groups, items, jnp.where(row == plan.groups, high, low))
    block_ref[base : base + PAD, :] = extra
    send_ref[base : base + PAD, :] = extra.astype(bf16)


def outer_body(plan, block_ref, head_ref, *refs):
    n = plan.outer
    got, (same_ref, flip_ref) = refs[: n - 1], refs[n - 1 :]
    inner = place_of()[3]
    base, stride, groups = plan.stacked, plan.block_rows, plan.groups
    total = block_ref[0:base, :]
    extras = [block_ref[base : base + PAD, :].astype(bf16).astype(f32)]
    for r in got:
        total = total + r[0:base, :].astype(f32)
        extras.append(r[base : base + PAD, :].astype(f32))
    row = lax.broadcasted_iota(jnp.int32, (PAD, LANES), 0)
    head_squares = jnp.zeros((1, LANES), f32)
    item_squares = jnp.zeros((PAD, LANES), f32)
    for extra in extras:
        head_squares = head_squares + extra[groups : groups + 1, :] + extra[groups + 1 : groups + 2, :]
        item_squares = item_squares + jnp.where(row < groups, extra * extra, 0.0)
    squares = (
        jnp.sum(jnp.sum(total * total, axis=1, keepdims=True), axis=0, keepdims=True)
        + jnp.sum(jnp.sum(item_squares, axis=1, keepdims=True), axis=0, keepdims=True)
        + head_squares
    )
    high, low = two_parts(jnp.broadcast_to(squares, (PAD, LANES)))
    items = jnp.concatenate([extra[0:groups, :] for extra in extras], axis=0).astype(bf16)
    sums = jnp.where(row == 0, high, low).astype(bf16)
    block = total.astype(bf16)
    for out, member in ((same_ref, inner), (flip_ref, 1 - inner)):
        at = pl.ds(pl.multiple_of(member * stride, stride), stride)
        out[0:base, :] = block
        out[base : base + groups * n, :] = items
        spot = base + groups * n
        out[spot : spot + stride, :] = head_ref[at, :].astype(bf16)
        out[spot + stride : spot + stride + PAD, :] = sums


def half_body(plan, had_ref, got_ref, keep_ref, send_ref):
    half = keep_ref.shape[0]
    keep_ref[...] = had_ref[0:half, :] + got_ref[0:half, :].astype(f32)
    send_ref[...] = (had_ref[half : 2 * half, :] + got_ref[half : 2 * half, :].astype(f32)).astype(bf16)


def back_body(plan, had_ref, got_ref, feat_ref, mean_ref):
    total = had_ref[...] + got_ref[...].astype(f32)
    feat_ref[...] = total[:, 0 : plan.width]
    mean_ref[...] = total[:, plan.width :] / plan.n_mem


def update_body(plan, *refs):
    chunks = refs[: plan.shards]
    states = refs[plan.shards : plan.shards + 10]
    outs = refs[plan.shards + 10 : plan.shards + 25]
    held, items_ref, sems = refs[plan.shards + 25 : -2], refs[-2], refs[-1]
    bw, bm, bv, vw, vm, vv, hw, hm, hv, cs = states
    norm_out, vec_outs, bias_outs, block_outs, head_outs = (
        outs[0],
        outs[5:8],
        outs[12:15],
        outs[1:5],
        outs[8:12],
    )
    norm_ref, vec_refs, bias_refs, block_refs, head_refs = (
        held[0],
        held[5:8],
        held[12:15],
        held[1:5],
        held[8:12],
    )
    core, quad, outer, inner = place_of()
    n, groups, stride, base = plan.outer, plan.groups, plan.block_rows, plan.stacked
    spot = base + groups * n
    copies = []

    def send(source, target):
        copies.append(pltpu.make_async_copy(source, target, sems.at[len(copies)]))
        copies[-1].start()

    squares = jnp.zeros((1, LANES), f32)
    for chunk in chunks:
        sums = chunk[spot + stride : spot + stride + PAD, :].astype(f32)
        squares = squares + sums[0:1, :] + sums[1:2, :]
    norm = jnp.sqrt(squares)
    norm_ref[...] = norm
    factor = clip_limit / jnp.maximum(norm, clip_limit)
    send(norm_ref, norm_out)

    def shard_of(i):
        side, k = divmod(i, plan.quads)
        return (core ^ side) * plan.quads + (quad ^ k)

    for i, chunk in enumerate(chunks):
        shard = shard_of(i)
        items = chunk[base : base + groups * n, :].astype(f32)
        for z in range(n):
            items_ref[shard // 2, (outer ^ z) * 2 + shard % 2] = items[z * groups : (z + 1) * groups, :]
    wide = jnp.concatenate([factor] * groups, axis=1)
    for t in range(3):
        grad = jnp.concatenate([items_ref[t, :, g, :] for g in range(groups)], axis=1) * wide
        for ref, v in zip(vec_refs, adamw(vw[t], grad, vm[t], vv[t], 0.5, 0.0)):
            ref[t] = v
    grad = items_ref[3, outer * 2 + inner, 0:1, :] * factor
    for ref, v in zip(bias_refs, adamw(cs[0:1, :], grad, cs[1:2, :], cs[2:3, :], 0.1, 0.0)):
        ref[...] = v
    for source, target in zip(vec_refs + bias_refs, vec_outs + bias_outs):
        send(source, target)

    for i, chunk in enumerate(chunks):
        at = pl.ds(pl.multiple_of(shard_of(i) * stride, stride), stride)
        for g in range(groups):
            lanes = slice(g * LANES, (g + 1) * LANES)
            grad = chunk[g * stride : (g + 1) * stride, :].astype(f32) * factor
            new = adamw(bw[at, lanes], grad, bm[at, lanes], bv[at, lanes], 0.02, 0.01)
            for ref, v in zip(block_refs, new + (new[0],)):
                ref[at, lanes] = v.astype(ref.dtype)
        grad = chunk[spot : spot + stride, :].astype(f32) * factor
        new = adamw(hw[at, :], grad, hm[at, :], hv[at, :], 0.02, 0.01)
        for ref, v in zip(head_refs, new + (new[0],)):
            ref[at, :] = v.astype(ref.dtype)
        if i % 2:
            both = pl.ds(pl.multiple_of(shard_of(i) // 2 * (2 * stride), 2 * stride), 2 * stride)
            for source, target in zip(block_refs + head_refs, block_outs + head_outs):
                send(source.at[both], target.at[both])
    for copy in copies:
        copy.wait()


def on_device(
    mesh,
    features,
    labels,
    block_weight,
    block_first,
    block_second,
    member_vectors,
    vectors_first,
    vectors_second,
    head_weight,
    head_first,
    head_second,
    head_bias,
    bias_first,
    bias_second,
):
    rows, width = features.shape
    classes = head_weight.shape[-1]
    plan = Plan(mesh, width, classes, rows)
    n, quads, stride = plan.outer, plan.quads, plan.block_rows
    shape = jax.ShapeDtypeStruct
    mem = lax.axis_index("mem")
    outer = mem // 2

    far_feats = [plan.over_outer(features, k) for k in range(1, n)]
    head_low = head_weight[0].astype(bf16)
    bias_low = jnp.broadcast_to(head_bias.astype(bf16), (PAD, classes))
    far_head = plan.over_plane(jnp.concatenate([head_low, bias_low], axis=0), 1)
    onehot = (
        jnp.arange(classes, dtype=jnp.int32)[None, :] == labels[:, None]
    ).astype(f32)
    weight_low = block_weight.astype(bf16)
    biases = jnp.concatenate([head_bias, bias_first, bias_second], axis=0)
    onehot, biases = lax.optimization_barrier((onehot, biases))
    pair = lax.dynamic_slice_in_dim(member_vectors, outer * 2, 2, axis=1).reshape(6, width)

    objs = n * rows
    total = plan.stacked + 2 * stride + PAD
    back = width + classes
    outs = call(
        functools.partial(local_body, plan),
        [
            shape((quads, total, LANES), bf16),
            shape((quads, total, LANES), f32),
            shape((objs // 2, back), f32),
            shape((objs // 2, back), bf16),
        ],
        [features, *far_feats, onehot, weight_low, pair, head_low, bias_low, far_head],
        [
            pltpu.VMEM((2 * objs, width), bf16),
            pltpu.VMEM((2 * objs, width), f32),
            pltpu.VMEM((2 * objs, width), bf16),
            pltpu.VMEM((2 * objs, width), f32),
            pltpu.VMEM((2 * objs, width), bf16),
            pltpu.VMEM((max(width, objs), width), f32),
            pltpu.VMEM((2, width, classes), f32),
            pltpu.VMEM((plan.items, PAD, LANES), f32),
        ],
        name="local",
    )
    send, keep, back_keep, back_send = outs

    got = plan.over_core(send)
    own, *sends = call(
        functools.partial(core_body, plan),
        [shape((total, LANES), f32)] + [shape((total, LANES), bf16)] * (quads - 1),
        [keep, got],
        name="core_sum",
    )
    got = [plan.over_plane(v, k + 1) for k, v in enumerate(sends)]
    for bit in plan.bits[:-1]:
        half = back_keep.shape[0] // 2
        back_keep, back_send = call(
            functools.partial(half_body, plan),
            [shape((half, back), f32), shape((half, back), bf16)],
            [back_keep, plan.over_outer(back_send, bit)],
            name="back_half",
        )
    got[0], back_send, back_keep = lax.optimization_barrier((got[0], back_send, back_keep))
    send, block, heads = call(
        functools.partial(plane_body, plan),
        [
            shape((plan.stacked + PAD, LANES), bf16),
            shape((plan.stacked + PAD, LANES), f32),
            shape((2 * stride, LANES), f32),
        ],
        [own, *got],
        name="plane_sum",
    )
    got = [plan.over_outer(send, k) for k in range(1, n)]
    features_grad, mean_logits = call(
        functools.partial(back_body, plan),
        [shape((rows, width), f32), shape((rows, classes), f32)],
        [back_keep, plan.over_outer(back_send, plan.bits[-1])],
        name="back_sum",
    )
    got, features_grad, mean_logits = lax.optimization_barrier((got, features_grad, mean_logits))
    last = plan.stacked + plan.groups * n + stride + PAD
    same, flip = call(
        functools.partial(outer_body, plan),
        [shape((last, LANES), bf16)] * 2,
        [block, heads, *got],
        name="outer_sum",
    )
    near = [same] + [plan.over_plane(flip if k & 1 else same, k) for k in range(1, quads)]
    far = [plan.over_core(v) for v in near]

    like = lambda v, dtype=f32: (v.shape, dtype)
    head_w, head_m, head_v = head_weight[0], head_first[0], head_second[0]
    results = (
        [((1, LANES), f32)]
        + [like(block_weight)] * 3
        + [like(block_weight, bf16)]
        + [like(member_vectors)] * 3
        + [like(head_w)] * 3
        + [like(head_w, bf16)]
        + [like(head_bias)] * 3
    )
    (norm, bw, bm, bv, bcopy, vw, vm, vv, hw, hm, hv, hcopy, cw, cm, cv) = call(
        functools.partial(update_body, plan),
        [shape(*r) for r in results],
        [
            *near,
            *far,
            block_weight,
            block_first,
            block_second,
            member_vectors,
            vectors_first,
            vectors_second,
            head_w,
            head_m,
            head_v,
            biases,
        ],
        [pltpu.VMEM(*r) for r in results]
        + [
            pltpu.VMEM((plan.items // 2, plan.n_mem, plan.groups, LANES), f32),
            pltpu.SemaphoreType.DMA((7 + 8 * plan.quads,)),
        ],
        name="update",
        out_spec=pl.BlockSpec(memory_space=pl.ANY),
    )
    return (
        mean_logits,
        features_grad,
        norm[0, 0],
        bw,
        bm,
        bv,
        bcopy,
        vw,
        vm,
        vv,
        hw[None],
        hm[None],
        hv[None],
        hcopy[None],
        cw,
        cm,
        cv,
    )


def solution(mesh):
    split, whole = P(ALL, None), P()
    heads, biases = P("mem", None, None), P("mem", None)
    return jax.shard_map(
        functools.partial(on_device, mesh),
        mesh=mesh,
        in_specs=(split, P("obj")) + (whole,) * 6 + (heads,) * 3 + (biases,) * 3,
        out_specs=(split, split) + (whole,) * 8 + (heads,) * 4 + (biases,) * 3,
        check_vma=False,
    )
```

```python
import functools
import math

import jax
import jax.numpy as jnp
from jax import lax
from jax.experimental import pallas as pl
from jax.experimental.pallas import tpu as pltpu
from jax.sharding import PartitionSpec as P

STEP = 5
ALL = ("obj", "mem")
LANES = 128
PAD = 16
MIB = 1 << 20

clip_limit = 100.0
beta_one = 0.5
beta_two = 0.5
epsilon = 1e-08
gelu_in = math.sqrt(2.0 / math.pi)
gelu_cube = 0.044715

bf16 = jnp.bfloat16
f32 = jnp.float32
VMEM = pl.BlockSpec(memory_space=pltpu.VMEM)
SMEM = pl.BlockSpec(memory_space=pltpu.SMEM)


def adamw(weight, grad, first, second, rate, decay):
    first_new = beta_one * first + (1.0 - beta_one) * grad
    second_new = beta_two * second + (1.0 - beta_two) * grad * grad
    fix_one = 1.0 / (1.0 - beta_one**STEP)
    fix_two = 1.0 / (1.0 - beta_two**STEP)
    root = lax.rsqrt(second_new * fix_two)
    step_size = first_new * root * (rate * fix_one) / (1.0 + epsilon * root)
    return (weight * (1.0 - rate * decay) - step_size, first_new, second_new)


def dot(a, b, dims=((1,), (0,))):
    return lax.dot_general(a, b, (dims, ((), ())), preferred_element_type=f32)


def call(body, outs, args, scratch=(), name=None, out_spec=VMEM):
    specs = [VMEM] * len(args)
    return pl.pallas_call(
        body,
        out_shape=outs,
        in_specs=specs,
        out_specs=[out_spec] * len(outs),
        scratch_shapes=list(scratch),
        compiler_params=pltpu.CompilerParams(vmem_limit_bytes=40 * MIB),
        name=name,
    )(*args)


class Plan:
    def __init__(self, mesh, width, classes, rows):
        self.n_obj, self.n_mem = mesh.shape["obj"], mesh.shape["mem"]
        self.outer = self.n_mem // 2
        self.quads = self.n_obj
        self.shards = 2 * self.quads
        self.width, self.classes, self.rows = width, classes, rows
        self.groups = width // LANES
        self.block_rows = width // self.shards
        self.stacked = self.block_rows * self.groups
        self.items = max(8, self.shards)
        self.bits = [1 << i for i in range(self.outer.bit_length() - 1)]
        self.halving = sorted(range(self.outer), key=lambda k: [k & bit for bit in self.bits])

    def perm(self, move):
        pairs = []
        for obj in range(self.n_obj):
            for mem in range(self.n_mem):
                to_obj, to_mem = move(obj, mem)
                pairs.append((obj * self.n_mem + mem, to_obj * self.n_mem + to_mem))
        return pairs

    def over_core(self, v):
        return lax.ppermute(v, ALL, self.perm(lambda o, m: (o ^ 1, m)))

    def over_plane(self, v, k):
        return lax.ppermute(v, ALL, self.perm(lambda o, m: (o ^ (k >> 1 << 1), m ^ (k & 1))))

    def over_outer(self, v, k):
        return lax.ppermute(v, ALL, self.perm(lambda o, m: (o, m ^ (k << 1))))


def head_body(plan, head_ref, bias_ref, low_ref):
    low_ref[0 : plan.width, :] = head_ref[...].astype(bf16)
    low_ref[plan.width :, :] = jnp.broadcast_to(bias_ref[...], (PAD, plan.classes)).astype(bf16)


def low_body(plan, weight_ref, bias_ref, first_ref, second_ref, low_ref, biases_ref):
    low_ref[...] = weight_ref[...].astype(bf16)
    for i, ref in enumerate((bias_ref, first_ref, second_ref)):
        biases_ref[i : i + 1, :] = ref[...]


def local_body(plan, *refs):
    n = plan.outer
    feats = refs[:n]
    onehot_ref, weight_ref, vec_ref, own_head, far_head = refs[n : n + 5]
    send_ref, keep_ref = refs[n + 5 : n + 7]
    back_keep, back_send = refs[n + 7 : n + 9]
    lifted_ref, mixed_ref, hidden_ref, slope_ref, dmixed_ref, block_ref, heads_ref, items_ref = refs[
        n + 9 :
    ]
    rows, width, classes = plan.rows, plan.width, plan.classes
    objs = n * rows
    core, quad, outer, inner = place_of()
    tile = 16

    def member(j):
        return pl.ds(outer * 2 + j, 1)

    for j in range(2):
        scale_r = vec_ref[0, member(j), :]
        for k in range(n):
            lifted_ref[j * objs + k * rows : j * objs + (k + 1) * rows, :] = (
                feats[k][...].astype(f32) * scale_r
            ).astype(bf16)
    mixed_ref[...] = dot(lifted_ref[...], weight_ref[...])

    items_ref[...] = jnp.zeros_like(items_ref)
    for j in range(2):
        scale_s = vec_ref[1, member(j), :]
        shift_b = vec_ref[2, member(j), :]

        def forward(t, carry):
            at = pl.ds(pl.multiple_of(j * objs + t * tile, tile), tile)
            pre = mixed_ref[at, :] * scale_s + shift_b
            square = pre * pre
            half = 0.5 + 0.5 * jnp.tanh(pre * (gelu_in + (gelu_in * gelu_cube) * square))
            hidden_ref[at, :] = (pre * half).astype(bf16)
            slope_ref[at, :] = half + (half - half * half) * (
                pre * (2.0 * gelu_in + (6.0 * gelu_in * gelu_cube) * square)
            )
            return carry

        lax.fori_loop(0, objs // tile, forward, 0, unroll=min(objs // tile, 16))

    logit_sum = None
    for j in range(2):
        mine = inner == j
        head = jnp.where(mine, own_head[0:width, :], far_head[0:width, :])
        bias = jnp.where(mine, own_head[width : width + 1, :], far_head[width : width + 1, :]).astype(f32)
        hidden = hidden_ref[j * objs : (j + 1) * objs, :]
        logits = dot(hidden, head) + bias
        logit_sum = logits if logit_sum is None else logit_sum + logits
        top = jnp.max(logits, axis=-1, keepdims=True)
        grown = jnp.exp(logits - top)
        soft = grown / jnp.sum(grown, axis=-1, keepdims=True)
        hot = jnp.concatenate(
            [
                onehot_ref[pl.ds(pl.multiple_of(((outer ^ k) * 2 + inner) * rows, rows), rows), :]
                for k in range(n)
            ],
            axis=0,
        )
        dlogits = soft - hot
        dlow = dlogits.astype(bf16)
        items_ref[6 + j, 0:1, :] = jnp.sum(dlogits, axis=0, keepdims=True)
        heads_ref[j] = dot(hidden, dlow, ((0,), (0,)))
        mixed_back = dot(dlow, head, ((1,), (1,)))
        block_ref[0:objs, :] = mixed_back
        scale_s = vec_ref[1, member(j), :]

        def backward(t, carry):
            s_sum, b_sum = carry
            at = pl.ds(pl.multiple_of(j * objs + t * tile, tile), tile)
            near = pl.ds(pl.multiple_of(t * tile, tile), tile)
            dpre = block_ref[near, :].astype(bf16).astype(f32) * slope_ref[at, :]
            dmixed_ref[at, :] = (dpre * scale_s).astype(bf16)
            return s_sum + dpre * mixed_ref[at, :], b_sum + dpre

        zero = jnp.zeros((tile, width), f32)
        s_sum, b_sum = lax.fori_loop(0, objs // tile, backward, (zero, zero), unroll=min(objs // tile, 16))
        s_grad = jnp.sum(s_sum, axis=0, keepdims=True)
        b_grad = jnp.sum(b_sum, axis=0, keepdims=True)
        for g in range(plan.groups):
            at = slice(g * LANES, (g + 1) * LANES)
            items_ref[2 + j, g : g + 1, :] = s_grad[:, at]
            items_ref[4 + j, g : g + 1, :] = b_grad[:, at]

    slope_ref[...] = dot(dmixed_ref[...], weight_ref[...], ((1,), (1,)))
    r_sums = [jnp.zeros((1, width), f32) for _ in range(2)]
    for spot, k in enumerate(plan.halving):
        feat = feats[k][...].astype(f32)
        back = None
        for j in range(2):
            lift_back = slope_ref[j * objs + k * rows : j * objs + (k + 1) * rows, :]
            r_sums[j] = r_sums[j] + jnp.sum(lift_back * feat, axis=0, keepdims=True)
            part = lift_back * vec_ref[0, member(j), :]
            back = part if back is None else back + part
        out = back_keep if spot < n // 2 else back_send
        at = slice(spot % (n // 2) * rows, (spot % (n // 2) + 1) * rows)
        out[at, 0:width] = back.astype(out.dtype)
        out[at, width : width + classes] = logit_sum[k * rows : (k + 1) * rows, :].astype(out.dtype)
    for j in range(2):
        for g in range(plan.groups):
            items_ref[j, g : g + 1, :] = r_sums[j][:, g * LANES : (g + 1) * LANES]

    stride = plan.block_rows
    half = width // 2
    for out, side in ((keep_ref, core), (send_ref, 1 - core)):
        part = dot(lifted_ref[:, pl.ds(pl.multiple_of(side * half, half), half)], dmixed_ref[...], ((0,), (0,)))
        for k in range(plan.quads):
            for g in range(plan.groups):
                out[quad ^ k, g * stride : (g + 1) * stride, :] = part[
                    k * stride : (k + 1) * stride, g * LANES : (g + 1) * LANES
                ].astype(out.dtype)
        for k in range(plan.quads):
            shard = side * plan.quads + (quad ^ k)
            at = pl.ds(pl.multiple_of(shard * stride, stride), stride)
            base = plan.stacked
            for j in range(2):
                out[k, base : base + stride, :] = heads_ref[j, at, :].astype(out.dtype)
                base += stride
            out[k, base : base + PAD, :] = items_ref[shard].astype(out.dtype)


def core_body(plan, keep_ref, got_ref, own_ref, *send_refs):
    own_ref[...] = keep_ref[0] + got_ref[0].astype(f32)
    for k in range(1, plan.quads):
        send_refs[k - 1][...] = (keep_ref[k] + got_ref[k].astype(f32)).astype(bf16)


def place_of():
    obj, mem = lax.axis_index("obj"), lax.axis_index("mem")
    return obj % 2, obj // 2 * 2 + mem % 2, mem // 2, mem % 2


def two_parts(v):
    high = v.astype(bf16).astype(f32)
    return high, v - high


def plane_body(plan, own_ref, *refs):
    got, (send_ref, block_ref, head_ref) = refs[: plan.quads - 1], refs[plan.quads - 1 :]
    total = own_ref[...]
    for r in got:
        total = total + r[...].astype(f32)
    base = plan.stacked
    block_ref[0:base, :] = total[0:base, :]
    send_ref[0:base, :] = total[0:base, :].astype(bf16)
    heads = total[base : base + 2 * plan.block_rows, :]
    head_ref[...] = heads
    squares = jnp.sum(jnp.sum(heads * heads, axis=1, keepdims=True), axis=0, keepdims=True)
    high, low = two_parts(jnp.broadcast_to(squares, (PAD, LANES)))
    items = total[base + 2 * plan.block_rows :, :]
    row = lax.broadcasted_iota(jnp.int32, (PAD, LANES), 0)
    extra = jnp.where(row < plan.groups, items, jnp.where(row == plan.groups, high, low))
    block_ref[base : base + PAD, :] = extra
    send_ref[base : base + PAD, :] = extra.astype(bf16)


def outer_body(plan, block_ref, head_ref, *refs):
    n = plan.outer
    got, (same_ref, flip_ref) = refs[: n - 1], refs[n - 1 :]
    inner = place_of()[3]
    base, stride, groups = plan.stacked, plan.block_rows, plan.groups
    total = block_ref[0:base, :]
    extras = [block_ref[base : base + PAD, :].astype(bf16).astype(f32)]
    for r in got:
        total = total + r[0:base, :].astype(f32)
        extras.append(r[base : base + PAD, :].astype(f32))
    row = lax.broadcasted_iota(jnp.int32, (PAD, LANES), 0)
    head_squares = jnp.zeros((1, LANES), f32)
    item_squares = jnp.zeros((PAD, LANES), f32)
    for extra in extras:
        head_squares = head_squares + extra[groups : groups + 1, :] + extra[groups + 1 : groups + 2, :]
        item_squares = item_squares + jnp.where(row < groups, extra * extra, 0.0)
    squares = (
        jnp.sum(jnp.sum(total * total, axis=1, keepdims=True), axis=0, keepdims=True)
        + jnp.sum(jnp.sum(item_squares, axis=1, keepdims=True), axis=0, keepdims=True)
        + head_squares
    )
    high, low = two_parts(jnp.broadcast_to(squares, (PAD, LANES)))
    items = jnp.concatenate([extra[0:groups, :] for extra in extras], axis=0).astype(bf16)
    sums = jnp.where(row == 0, high, low).astype(bf16)
    block = total.astype(bf16)
    for out, member in ((same_ref, inner), (flip_ref, 1 - inner)):
        at = pl.ds(pl.multiple_of(member * stride, stride), stride)
        out[0:base, :] = block
        out[base : base + groups * n, :] = items
        spot = base + groups * n
        out[spot : spot + stride, :] = head_ref[at, :].astype(bf16)
        out[spot + stride : spot + stride + PAD, :] = sums


def half_body(plan, had_ref, got_ref, keep_ref, send_ref):
    half = keep_ref.shape[0]
    keep_ref[...] = had_ref[0:half, :] + got_ref[0:half, :].astype(f32)
    send_ref[...] = (had_ref[half : 2 * half, :] + got_ref[half : 2 * half, :].astype(f32)).astype(bf16)


def back_body(plan, had_ref, got_ref, feat_ref, mean_ref):
    total = had_ref[...] + got_ref[...].astype(f32)
    feat_ref[...] = total[:, 0 : plan.width]
    mean_ref[...] = total[:, plan.width :] / plan.n_mem


def update_body(plan, *refs):
    chunks = refs[: plan.shards]
    states = refs[plan.shards : plan.shards + 10]
    outs = refs[plan.shards + 10 : plan.shards + 25]
    held, items_ref, sems = refs[plan.shards + 25 : -2], refs[-2], refs[-1]
    bw, bm, bv, vw, vm, vv, hw, hm, hv, cs = states
    norm_out, vec_outs, bias_outs, block_outs, head_outs = (
        outs[0],
        outs[5:8],
        outs[12:15],
        outs[1:5],
        outs[8:12],
    )
    norm_ref, vec_refs, bias_refs, block_refs, head_refs = (
        held[0],
        held[5:8],
        held[12:15],
        held[1:5],
        held[8:12],
    )
    core, quad, outer, inner = place_of()
    n, groups, stride, base = plan.outer, plan.groups, plan.block_rows, plan.stacked
    spot = base + groups * n
    copies = []

    def send(source, target):
        copies.append(pltpu.make_async_copy(source, target, sems.at[len(copies)]))
        copies[-1].start()

    squares = jnp.zeros((1, LANES), f32)
    for chunk in chunks:
        sums = chunk[spot + stride : spot + stride + PAD, :].astype(f32)
        squares = squares + sums[0:1, :] + sums[1:2, :]
    norm = jnp.sqrt(squares)
    norm_ref[...] = norm
    factor = clip_limit / jnp.maximum(norm, clip_limit)
    send(norm_ref, norm_out)

    def shard_of(i):
        side, k = divmod(i, plan.quads)
        return (core ^ side) * plan.quads + (quad ^ k)

    for i, chunk in enumerate(chunks):
        at = pl.ds(pl.multiple_of(shard_of(i) * stride, stride), stride)
        for g in range(groups):
            lanes = slice(g * LANES, (g + 1) * LANES)
            grad = chunk[g * stride : (g + 1) * stride, :].astype(f32) * factor
            new = adamw(bw[at, lanes], grad, bm[at, lanes], bv[at, lanes], 0.02, 0.01)
            for ref, v in zip(block_refs, new + (new[0],)):
                ref[at, lanes] = v.astype(ref.dtype)
        grad = chunk[spot : spot + stride, :].astype(f32) * factor
        new = adamw(hw[at, :], grad, hm[at, :], hv[at, :], 0.02, 0.01)
        for ref, v in zip(head_refs, new + (new[0],)):
            ref[at, :] = v.astype(ref.dtype)
        if i % 2:
            both = pl.ds(pl.multiple_of(shard_of(i) // 2 * (2 * stride), 2 * stride), 2 * stride)
            for source, target in zip(block_refs + head_refs, block_outs + head_outs):
                send(source.at[both], target.at[both])
    for i, chunk in enumerate(chunks):
        shard = shard_of(i)
        items = chunk[base : base + groups * n, :].astype(f32)
        for z in range(n):
            items_ref[shard // 2, (outer ^ z) * 2 + shard % 2] = items[z * groups : (z + 1) * groups, :]
    wide = jnp.concatenate([factor] * groups, axis=1)
    for t in range(3):
        grad = jnp.concatenate([items_ref[t, :, g, :] for g in range(groups)], axis=1) * wide
        for ref, v in zip(vec_refs, adamw(vw[t], grad, vm[t], vv[t], 0.5, 0.0)):
            ref[t] = v
    grad = items_ref[3, outer * 2 + inner, 0:1, :] * factor
    for ref, v in zip(bias_refs, adamw(cs[0:1, :], grad, cs[1:2, :], cs[2:3, :], 0.1, 0.0)):
        ref[...] = v
    for source, target in zip(vec_refs + bias_refs, vec_outs + bias_outs):
        send(source, target)

    for copy in copies:
        copy.wait()


def on_device(
    mesh,
    features,
    labels,
    block_weight,
    block_first,
    block_second,
    member_vectors,
    vectors_first,
    vectors_second,
    head_weight,
    head_first,
    head_second,
    head_bias,
    bias_first,
    bias_second,
):
    rows, width = features.shape
    classes = head_weight.shape[-1]
    plan = Plan(mesh, width, classes, rows)
    n, quads, stride = plan.outer, plan.quads, plan.block_rows
    shape = jax.ShapeDtypeStruct

    far_feats = [plan.over_outer(features, k) for k in range(1, n)]
    (own_head,) = call(
        functools.partial(head_body, plan),
        [shape((width + PAD, classes), bf16)],
        [head_weight[0], head_bias],
        name="head_low",
    )
    far_head = plan.over_plane(own_head, 1)
    weight_low, biases = call(
        functools.partial(low_body, plan),
        [shape((width, width), bf16), shape((3, classes), f32)],
        [block_weight, head_bias, bias_first, bias_second],
        name="weight_low",
    )
    onehot = (
        jnp.arange(classes, dtype=jnp.int32)[None, :] == labels[:, None]
    ).astype(f32)

    objs = n * rows
    total = plan.stacked + 2 * stride + PAD
    back = width + classes
    outs = call(
        functools.partial(local_body, plan),
        [
            shape((quads, total, LANES), bf16),
            shape((quads, total, LANES), f32),
            shape((objs // 2, back), f32),
            shape((objs // 2, back), bf16),
        ],
        [features, *far_feats, onehot, weight_low, member_vectors, own_head, far_head],
        [
            pltpu.VMEM((2 * objs, width), bf16),
            pltpu.VMEM((2 * objs, width), f32),
            pltpu.VMEM((2 * objs, width), bf16),
            pltpu.VMEM((2 * objs, width), f32),
            pltpu.VMEM((2 * objs, width), bf16),
            pltpu.VMEM((max(width, objs), width), f32),
            pltpu.VMEM((2, width, classes), f32),
            pltpu.VMEM((plan.items, PAD, LANES), f32),
        ],
        name="local",
    )
    send, keep, back_keep, back_send = outs

    got = plan.over_core(send)
    own, *sends = call(
        functools.partial(core_body, plan),
        [shape((total, LANES), f32)] + [shape((total, LANES), bf16)] * (quads - 1),
        [keep, got],
        name="core_sum",
    )
    got = [plan.over_plane(v, k + 1) for k, v in enumerate(sends)]
    for bit in plan.bits[:-1]:
        half = back_keep.shape[0] // 2
        back_keep, back_send = call(
            functools.partial(half_body, plan),
            [shape((half, back), f32), shape((half, back), bf16)],
            [back_keep, plan.over_outer(back_send, bit)],
            name="back_half",
        )
    got[0], back_send, back_keep = lax.optimization_barrier((got[0], back_send, back_keep))
    send, block, heads = call(
        functools.partial(plane_body, plan),
        [
            shape((plan.stacked + PAD, LANES), bf16),
            shape((plan.stacked + PAD, LANES), f32),
            shape((2 * stride, LANES), f32),
        ],
        [own, *got],
        name="plane_sum",
    )
    got = [plan.over_outer(send, k) for k in range(1, n)]
    features_grad, mean_logits = call(
        functools.partial(back_body, plan),
        [shape((rows, width), f32), shape((rows, classes), f32)],
        [back_keep, plan.over_outer(back_send, plan.bits[-1])],
        name="back_sum",
    )
    got, features_grad, mean_logits = lax.optimization_barrier((got, features_grad, mean_logits))
    last = plan.stacked + plan.groups * n + stride + PAD
    same, flip = call(
        functools.partial(outer_body, plan),
        [shape((last, LANES), bf16)] * 2,
        [block, heads, *got],
        name="outer_sum",
    )
    near = [same] + [plan.over_plane(flip if k & 1 else same, k) for k in range(1, quads)]
    far = [plan.over_core(v) for v in near]

    like = lambda v, dtype=f32: (v.shape, dtype)
    head_w, head_m, head_v = head_weight[0], head_first[0], head_second[0]
    results = (
        [((1, LANES), f32)]
        + [like(block_weight)] * 3
        + [like(block_weight, bf16)]
        + [like(member_vectors)] * 3
        + [like(head_w)] * 3
        + [like(head_w, bf16)]
        + [like(head_bias)] * 3
    )
    (norm, bw, bm, bv, bcopy, vw, vm, vv, hw, hm, hv, hcopy, cw, cm, cv) = call(
        functools.partial(update_body, plan),
        [shape(*r) for r in results],
        [
            *near,
            *far,
            block_weight,
            block_first,
            block_second,
            member_vectors,
            vectors_first,
            vectors_second,
            head_w,
            head_m,
            head_v,
            biases,
        ],
        [pltpu.VMEM(*r) for r in results]
        + [
            pltpu.VMEM((plan.items // 2, plan.n_mem, plan.groups, LANES), f32),
            pltpu.SemaphoreType.DMA((7 + 8 * plan.quads,)),
        ],
        name="update",
        out_spec=pl.BlockSpec(memory_space=pl.ANY),
    )
    return (
        mean_logits,
        features_grad,
        norm[0, 0],
        bw,
        bm,
        bv,
        bcopy,
        vw,
        vm,
        vv,
        hw[None],
        hm[None],
        hv[None],
        hcopy[None],
        cw,
        cm,
        cv,
    )


def solution(mesh):
    split, whole = P(ALL, None), P()
    heads, biases = P("mem", None, None), P("mem", None)
    return jax.shard_map(
        functools.partial(on_device, mesh),
        mesh=mesh,
        in_specs=(split, P("obj")) + (whole,) * 6 + (heads,) * 3 + (biases,) * 3,
        out_specs=(split, split) + (whole,) * 8 + (heads,) * 4 + (biases,) * 3,
        check_vma=False,
    )
```

```python
import functools
import math

import jax
import jax.numpy as jnp
from jax import lax
from jax.experimental import pallas as pl
from jax.experimental.pallas import tpu as pltpu
from jax.sharding import PartitionSpec as P

STEP = 5
ALL = ("obj", "mem")
LANES = 128
PAD = 16
MIB = 1 << 20

clip_limit = 100.0
beta_one = 0.5
beta_two = 0.5
epsilon = 1e-08
gelu_in = math.sqrt(2.0 / math.pi)
gelu_cube = 0.044715

bf16 = jnp.bfloat16
f32 = jnp.float32
VMEM = pl.BlockSpec(memory_space=pltpu.VMEM)
SMEM = pl.BlockSpec(memory_space=pltpu.SMEM)


def adamw(weight, grad, first, second, rate, decay):
    first_new = beta_one * first + (1.0 - beta_one) * grad
    second_new = beta_two * second + (1.0 - beta_two) * grad * grad
    fix_one = 1.0 / (1.0 - beta_one**STEP)
    fix_two = 1.0 / (1.0 - beta_two**STEP)
    root = lax.rsqrt(second_new * fix_two)
    step_size = first_new * root * (rate * fix_one) / (1.0 + epsilon * root)
    return (weight * (1.0 - rate * decay) - step_size, first_new, second_new)


def dot(a, b, dims=((1,), (0,))):
    return lax.dot_general(a, b, (dims, ((), ())), preferred_element_type=f32)


def call(body, outs, args, scratch=(), name=None, out_spec=VMEM, aliases=None, in_hbm=()):
    specs = [pl.BlockSpec(memory_space=pl.ANY) if i in in_hbm else VMEM for i in range(len(args))]
    return pl.pallas_call(
        body,
        out_shape=outs,
        in_specs=specs,
        out_specs=[out_spec] * len(outs),
        scratch_shapes=list(scratch),
        input_output_aliases=aliases or {},
        compiler_params=pltpu.CompilerParams(vmem_limit_bytes=40 * MIB),
        name=name,
    )(*args)


class Plan:
    def __init__(self, mesh, width, classes, rows):
        self.n_obj, self.n_mem = mesh.shape["obj"], mesh.shape["mem"]
        self.outer = self.n_mem // 2
        self.quads = self.n_obj
        self.shards = 2 * self.quads
        self.width, self.classes, self.rows = width, classes, rows
        self.groups = width // LANES
        self.block_rows = width // self.shards
        self.stacked = self.block_rows * self.groups
        self.items = max(8, self.shards)
        self.bits = [1 << i for i in range(self.outer.bit_length() - 1)]
        self.halving = sorted(range(self.outer), key=lambda k: [k & bit for bit in self.bits])

    def perm(self, move):
        pairs = []
        for obj in range(self.n_obj):
            for mem in range(self.n_mem):
                to_obj, to_mem = move(obj, mem)
                pairs.append((obj * self.n_mem + mem, to_obj * self.n_mem + to_mem))
        return pairs

    def over_core(self, v):
        return lax.ppermute(v, ALL, self.perm(lambda o, m: (o ^ 1, m)))

    def over_plane(self, v, k):
        return lax.ppermute(v, ALL, self.perm(lambda o, m: (o ^ (k >> 1 << 1), m ^ (k & 1))))

    def over_outer(self, v, k):
        return lax.ppermute(v, ALL, self.perm(lambda o, m: (o, m ^ (k << 1))))


def head_body(plan, head_ref, bias_ref, low_ref, held_ref, sem):
    copy = pltpu.make_async_copy(bias_ref, held_ref, sem)
    copy.start()
    low_ref[0 : plan.width, :] = head_ref[...].astype(bf16)
    copy.wait()
    low_ref[plan.width :, :] = jnp.broadcast_to(held_ref[...], (PAD, plan.classes)).astype(bf16)


def low_body(plan, weight_ref, bias_ref, first_ref, second_ref, low_ref, biases_ref):
    low_ref[...] = weight_ref[...].astype(bf16)
    for i, ref in enumerate((bias_ref, first_ref, second_ref)):
        biases_ref[i : i + 1, :] = ref[...]


def forward_body(plan, pieces, *refs):
    feats, (weight_ref, vec_ref) = refs[: len(pieces)], refs[len(pieces) : len(pieces) + 2]
    lifted_ref, mixed_ref, hidden_ref, slope_ref = refs[-4:]
    rows, objs = plan.rows, plan.outer * plan.rows
    outer = place_of()[2]
    tile = 16
    for j in range(2):
        scale_r, scale_s, shift_b = (vec_ref[t, pl.ds(outer * 2 + j, 1), :] for t in range(3))
        first, last = j * objs + pieces[0] * rows, j * objs + (pieces[-1] + 1) * rows
        for k, feat in zip(pieces, feats):
            lifted_ref[j * objs + k * rows : j * objs + (k + 1) * rows, :] = (
                feat[...].astype(f32) * scale_r
            ).astype(bf16)
        mixed_ref[first:last, :] = dot(lifted_ref[first:last, :], weight_ref[...])

        def forward(t, carry):
            at = pl.ds(pl.multiple_of(first + t * tile, tile), tile)
            pre = mixed_ref[at, :] * scale_s + shift_b
            square = pre * pre
            half = 0.5 + 0.5 * jnp.tanh(pre * (gelu_in + (gelu_in * gelu_cube) * square))
            hidden_ref[at, :] = (pre * half).astype(bf16)
            slope_ref[at, :] = half + (half - half * half) * (
                pre * (2.0 * gelu_in + (6.0 * gelu_in * gelu_cube) * square)
            )
            return carry

        steps = (last - first) // tile
        lax.fori_loop(0, steps, forward, 0, unroll=min(steps, 16))


def local_body(plan, *refs):
    n = plan.outer
    feats = refs[:n]
    onehot_ref, weight_ref, vec_ref, own_head, far_head = refs[n : n + 5]
    lifted_ref, mixed_ref, hidden_ref, slope_ref = refs[n + 5 : n + 9]
    send_ref, keep_ref, back_keep, back_send = refs[n + 9 : n + 13]
    dmixed_ref, block_ref, heads_ref, items_ref = refs[n + 13 :]
    rows, width, classes = plan.rows, plan.width, plan.classes
    objs = n * rows
    core, quad, outer, inner = place_of()
    tile = 16

    def member(j):
        return pl.ds(outer * 2 + j, 1)

    items_ref[...] = jnp.zeros_like(items_ref)
    logit_sum = None
    for j in range(2):
        mine = inner == j
        head = jnp.where(mine, own_head[0:width, :], far_head[0:width, :])
        bias = jnp.where(mine, own_head[width : width + 1, :], far_head[width : width + 1, :]).astype(f32)
        hidden = hidden_ref[j * objs : (j + 1) * objs, :]
        logits = dot(hidden, head) + bias
        logit_sum = logits if logit_sum is None else logit_sum + logits
        top = jnp.max(logits, axis=-1, keepdims=True)
        grown = jnp.exp(logits - top)
        soft = grown / jnp.sum(grown, axis=-1, keepdims=True)
        hot = jnp.concatenate(
            [
                onehot_ref[pl.ds(pl.multiple_of(((outer ^ (-p % n)) * 2 + inner) * rows, rows), rows), :]
                for p in range(n)
            ],
            axis=0,
        )
        dlogits = soft - hot
        dlow = dlogits.astype(bf16)
        items_ref[6 + j, 0:1, :] = jnp.sum(dlogits, axis=0, keepdims=True)
        heads_ref[j] = dot(hidden, dlow, ((0,), (0,)))
        mixed_back = dot(dlow, head, ((1,), (1,)))
        block_ref[0:objs, :] = mixed_back
        scale_s = vec_ref[1, member(j), :]

        def backward(t, carry):
            s_sum, b_sum = carry
            at = pl.ds(pl.multiple_of(j * objs + t * tile, tile), tile)
            near = pl.ds(pl.multiple_of(t * tile, tile), tile)
            dpre = block_ref[near, :].astype(bf16).astype(f32) * slope_ref[at, :]
            dmixed_ref[at, :] = (dpre * scale_s).astype(bf16)
            return s_sum + dpre * mixed_ref[at, :], b_sum + dpre

        zero = jnp.zeros((tile, width), f32)
        s_sum, b_sum = lax.fori_loop(0, objs // tile, backward, (zero, zero), unroll=min(objs // tile, 16))
        s_grad = jnp.sum(s_sum, axis=0, keepdims=True)
        b_grad = jnp.sum(b_sum, axis=0, keepdims=True)
        for g in range(plan.groups):
            at = slice(g * LANES, (g + 1) * LANES)
            items_ref[2 + j, g : g + 1, :] = s_grad[:, at]
            items_ref[4 + j, g : g + 1, :] = b_grad[:, at]

    block_ref[...] = dot(dmixed_ref[...], weight_ref[...], ((1,), (1,)))
    r_sums = [jnp.zeros((1, width), f32) for _ in range(2)]
    for spot, k in enumerate(plan.halving):
        p = -k % n
        feat = feats[k][...].astype(f32)
        back = None
        for j in range(2):
            lift_back = block_ref[j * objs + p * rows : j * objs + (p + 1) * rows, :]
            r_sums[j] = r_sums[j] + jnp.sum(lift_back * feat, axis=0, keepdims=True)
            part = lift_back * vec_ref[0, member(j), :]
            back = part if back is None else back + part
        out = back_keep if spot < n // 2 else back_send
        at = slice(spot % (n // 2) * rows, (spot % (n // 2) + 1) * rows)
        out[at, 0:width] = back.astype(out.dtype)
        out[at, width : width + classes] = logit_sum[p * rows : (p + 1) * rows, :].astype(out.dtype)
    for j in range(2):
        for g in range(plan.groups):
            items_ref[j, g : g + 1, :] = r_sums[j][:, g * LANES : (g + 1) * LANES]

    stride = plan.block_rows
    half = width // 2
    for out, side in ((keep_ref, core), (send_ref, 1 - core)):
        part = dot(lifted_ref[:, pl.ds(pl.multiple_of(side * half, half), half)], dmixed_ref[...], ((0,), (0,)))
        for k in range(plan.quads):
            for g in range(plan.groups):
                out[quad ^ k, g * stride : (g + 1) * stride, :] = part[
                    k * stride : (k + 1) * stride, g * LANES : (g + 1) * LANES
                ].astype(out.dtype)
        for k in range(plan.quads):
            shard = side * plan.quads + (quad ^ k)
            at = pl.ds(pl.multiple_of(shard * stride, stride), stride)
            base = plan.stacked
            for j in range(2):
                out[k, base : base + stride, :] = heads_ref[j, at, :].astype(out.dtype)
                base += stride
            out[k, base : base + PAD, :] = items_ref[shard].astype(out.dtype)


def core_body(plan, keep_ref, got_ref, own_ref, *send_refs):
    own_ref[...] = keep_ref[0] + got_ref[0].astype(f32)
    for k in range(1, plan.quads):
        send_refs[k - 1][...] = (keep_ref[k] + got_ref[k].astype(f32)).astype(bf16)


def place_of():
    obj, mem = lax.axis_index("obj"), lax.axis_index("mem")
    return obj % 2, obj // 2 * 2 + mem % 2, mem // 2, mem % 2


def two_parts(v):
    high = v.astype(bf16).astype(f32)
    return high, v - high


def plane_body(plan, own_ref, *refs):
    got, (send_ref, block_ref, head_ref) = refs[: plan.quads - 1], refs[plan.quads - 1 :]
    total = own_ref[...]
    for r in got:
        total = total + r[...].astype(f32)
    base = plan.stacked
    block_ref[0:base, :] = total[0:base, :]
    send_ref[0:base, :] = total[0:base, :].astype(bf16)
    heads = total[base : base + 2 * plan.block_rows, :]
    head_ref[...] = heads
    squares = jnp.sum(jnp.sum(heads * heads, axis=1, keepdims=True), axis=0, keepdims=True)
    high, low = two_parts(jnp.broadcast_to(squares, (PAD, LANES)))
    items = total[base + 2 * plan.block_rows :, :]
    row = lax.broadcasted_iota(jnp.int32, (PAD, LANES), 0)
    extra = jnp.where(row < plan.groups, items, jnp.where(row == plan.groups, high, low))
    block_ref[base : base + PAD, :] = extra
    send_ref[base : base + PAD, :] = extra.astype(bf16)


def outer_body(plan, block_ref, head_ref, *refs):
    n = plan.outer
    got, (same_ref, flip_ref) = refs[: n - 1], refs[n - 1 :]
    inner = place_of()[3]
    base, stride, groups = plan.stacked, plan.block_rows, plan.groups
    total = block_ref[0:base, :]
    extras = [block_ref[base : base + PAD, :].astype(bf16).astype(f32)]
    for r in got:
        total = total + r[0:base, :].astype(f32)
        extras.append(r[base : base + PAD, :].astype(f32))
    row = lax.broadcasted_iota(jnp.int32, (PAD, LANES), 0)
    head_squares = jnp.zeros((1, LANES), f32)
    item_squares = jnp.zeros((PAD, LANES), f32)
    for extra in extras:
        head_squares = head_squares + extra[groups : groups + 1, :] + extra[groups + 1 : groups + 2, :]
        item_squares = item_squares + jnp.where(row < groups, extra * extra, 0.0)
    squares = (
        jnp.sum(jnp.sum(total * total, axis=1, keepdims=True), axis=0, keepdims=True)
        + jnp.sum(jnp.sum(item_squares, axis=1, keepdims=True), axis=0, keepdims=True)
        + head_squares
    )
    high, low = two_parts(jnp.broadcast_to(squares, (PAD, LANES)))
    items = jnp.concatenate([extra[0:groups, :] for extra in extras], axis=0).astype(bf16)
    sums = jnp.where(row == 0, high, low).astype(bf16)
    block = total.astype(bf16)
    for out, member in ((same_ref, inner), (flip_ref, 1 - inner)):
        at = pl.ds(pl.multiple_of(member * stride, stride), stride)
        out[0:base, :] = block
        out[base : base + groups * n, :] = items
        spot = base + groups * n
        out[spot : spot + stride, :] = head_ref[at, :].astype(bf16)
        out[spot + stride : spot + stride + PAD, :] = sums


def half_body(plan, had_ref, got_ref, keep_ref, send_ref):
    half = keep_ref.shape[0]
    keep_ref[...] = had_ref[0:half, :] + got_ref[0:half, :].astype(f32)
    send_ref[...] = (had_ref[half : 2 * half, :] + got_ref[half : 2 * half, :].astype(f32)).astype(bf16)


def back_body(plan, had_ref, got_ref, feat_ref, mean_ref):
    total = had_ref[...] + got_ref[...].astype(f32)
    feat_ref[...] = total[:, 0 : plan.width]
    mean_ref[...] = total[:, plan.width :] / plan.n_mem


def update_body(plan, *refs):
    chunks = refs[: plan.shards]
    states = refs[plan.shards : plan.shards + 10]
    outs = refs[plan.shards + 10 : plan.shards + 25]
    held, items_ref, sems = refs[plan.shards + 25 : -2], refs[-2], refs[-1]
    bw, bm, bv, vw, vm, vv, hw, hm, hv, cs = states
    norm_out, vec_outs, bias_outs, block_outs, head_outs = (
        outs[0],
        outs[5:8],
        outs[12:15],
        outs[1:5],
        outs[8:12],
    )
    norm_ref, vec_refs, bias_refs, block_refs, head_refs = (
        held[0],
        held[5:8],
        held[12:15],
        held[1:5],
        held[8:12],
    )
    core, quad, outer, inner = place_of()
    n, groups, stride, base = plan.outer, plan.groups, plan.block_rows, plan.stacked
    spot = base + groups * n
    copies = []

    def send(source, target):
        copies.append(pltpu.make_async_copy(source, target, sems.at[len(copies)]))
        copies[-1].start()

    squares = jnp.zeros((1, LANES), f32)
    for chunk in chunks:
        sums = chunk[spot + stride : spot + stride + PAD, :].astype(f32)
        squares = squares + sums[0:1, :] + sums[1:2, :]
    norm = jnp.sqrt(squares)
    norm_ref[...] = norm
    factor = clip_limit / jnp.maximum(norm, clip_limit)
    send(norm_ref, norm_out)

    def shard_of(i):
        side, k = divmod(i, plan.quads)
        return (core ^ side) * plan.quads + (quad ^ k)

    for i, chunk in enumerate(chunks):
        at = pl.ds(pl.multiple_of(shard_of(i) * stride, stride), stride)
        for g in range(groups):
            lanes = slice(g * LANES, (g + 1) * LANES)
            grad = chunk[g * stride : (g + 1) * stride, :].astype(f32) * factor
            new = adamw(bw[at, lanes], grad, bm[at, lanes], bv[at, lanes], 0.02, 0.01)
            for ref, v in zip(block_refs, new + (new[0],)):
                ref[at, lanes] = v.astype(ref.dtype)
        grad = chunk[spot : spot + stride, :].astype(f32) * factor
        new = adamw(hw[at, :], grad, hm[at, :], hv[at, :], 0.02, 0.01)
        for ref, v in zip(head_refs, new + (new[0],)):
            ref[at, :] = v.astype(ref.dtype)
        if i % 2:
            both = pl.ds(pl.multiple_of(shard_of(i) // 2 * (2 * stride), 2 * stride), 2 * stride)
            for source, target in zip(block_refs + head_refs, block_outs + head_outs):
                send(source.at[both], target.at[both])
    for i, chunk in enumerate(chunks):
        shard = shard_of(i)
        items = chunk[base : base + groups * n, :].astype(f32)
        for z in range(n):
            items_ref[shard // 2, (outer ^ z) * 2 + shard % 2] = items[z * groups : (z + 1) * groups, :]
    wide = jnp.concatenate([factor] * groups, axis=1)
    for t in range(3):
        grad = jnp.concatenate([items_ref[t, :, g, :] for g in range(groups)], axis=1) * wide
        for ref, v in zip(vec_refs, adamw(vw[t], grad, vm[t], vv[t], 0.5, 0.0)):
            ref[t] = v
    grad = items_ref[3, outer * 2 + inner, 0:1, :] * factor
    for ref, v in zip(bias_refs, adamw(cs[0:1, :], grad, cs[1:2, :], cs[2:3, :], 0.1, 0.0)):
        ref[...] = v
    for source, target in zip(vec_refs + bias_refs, vec_outs + bias_outs):
        send(source, target)

    for copy in copies:
        copy.wait()


def on_device(
    mesh,
    features,
    labels,
    block_weight,
    block_first,
    block_second,
    member_vectors,
    vectors_first,
    vectors_second,
    head_weight,
    head_first,
    head_second,
    head_bias,
    bias_first,
    bias_second,
):
    rows, width = features.shape
    classes = head_weight.shape[-1]
    plan = Plan(mesh, width, classes, rows)
    n, quads, stride = plan.outer, plan.quads, plan.block_rows
    shape = jax.ShapeDtypeStruct

    far_feats = [plan.over_outer(features, k) for k in range(n - 1, 0, -1)][::-1]
    (own_head,) = call(
        functools.partial(head_body, plan),
        [shape((width + PAD, classes), bf16)],
        [head_weight[0], head_bias],
        [pltpu.VMEM(head_bias.shape, f32), pltpu.SemaphoreType.DMA],
        name="head_low",
        in_hbm=(1,),
    )
    far_head = plan.over_plane(own_head, 1)
    weight_low, biases = call(
        functools.partial(low_body, plan),
        [shape((width, width), bf16), shape((3, classes), f32)],
        [block_weight, head_bias, bias_first, bias_second],
        name="weight_low",
    )
    onehot = (
        jnp.arange(classes, dtype=jnp.int32)[None, :] == labels[:, None]
    ).astype(f32)

    objs = n * rows
    total = plan.stacked + 2 * stride + PAD
    back = width + classes
    done = ()
    for pieces in (range(n),):
        done = call(
            functools.partial(forward_body, plan, pieces),
            [shape((2 * objs, width), dtype) for dtype in (bf16, f32, bf16, f32)],
            [([features] + far_feats)[-k] for k in pieces] + [weight_low, member_vectors, *done],
            name="forward",
            aliases={3 + i: i for i in range(len(done))},
        )
    outs = call(
        functools.partial(local_body, plan),
        [
            shape((quads, total, LANES), bf16),
            shape((quads, total, LANES), f32),
            shape((objs // 2, back), f32),
            shape((objs // 2, back), bf16),
        ],
        [features, *far_feats, onehot, weight_low, member_vectors, own_head, far_head, *done],
        [
            pltpu.VMEM((2 * objs, width), bf16),
            pltpu.VMEM((2 * objs, width), f32),
            pltpu.VMEM((2, width, classes), f32),
            pltpu.VMEM((plan.items, PAD, LANES), f32),
        ],
        name="local",
    )
    send, keep, back_keep, back_send = outs

    got = plan.over_core(send)
    own, *sends = call(
        functools.partial(core_body, plan),
        [shape((total, LANES), f32)] + [shape((total, LANES), bf16)] * (quads - 1),
        [keep, got],
        name="core_sum",
    )
    got = [plan.over_plane(v, k + 1) for k, v in enumerate(sends)]
    for bit in plan.bits[:-1]:
        half = back_keep.shape[0] // 2
        back_keep, back_send = call(
            functools.partial(half_body, plan),
            [shape((half, back), f32), shape((half, back), bf16)],
            [back_keep, plan.over_outer(back_send, bit)],
            name="back_half",
        )
    own, back_send, back_keep = lax.optimization_barrier((own, back_send, back_keep))
    send, block, heads = call(
        functools.partial(plane_body, plan),
        [
            shape((plan.stacked + PAD, LANES), bf16),
            shape((plan.stacked + PAD, LANES), f32),
            shape((2 * stride, LANES), f32),
        ],
        [own, *got],
        name="plane_sum",
    )
    got = [plan.over_outer(send, k) for k in range(1, n)]
    features_grad, mean_logits = call(
        functools.partial(back_body, plan),
        [shape((rows, width), f32), shape((rows, classes), f32)],
        [back_keep, plan.over_outer(back_send, plan.bits[-1])],
        name="back_sum",
    )
    got, features_grad, mean_logits = lax.optimization_barrier((got, features_grad, mean_logits))
    last = plan.stacked + plan.groups * n + stride + PAD
    same, flip = call(
        functools.partial(outer_body, plan),
        [shape((last, LANES), bf16)] * 2,
        [block, heads, *got],
        name="outer_sum",
    )
    near = [same] + [plan.over_plane(flip if k & 1 else same, k) for k in range(1, quads)]
    far = [plan.over_core(v) for v in near]

    like = lambda v, dtype=f32: (v.shape, dtype)
    head_w, head_m, head_v = head_weight[0], head_first[0], head_second[0]
    results = (
        [((1, LANES), f32)]
        + [like(block_weight)] * 3
        + [like(block_weight, bf16)]
        + [like(member_vectors)] * 3
        + [like(head_w)] * 3
        + [like(head_w, bf16)]
        + [like(head_bias)] * 3
    )
    (norm, bw, bm, bv, bcopy, vw, vm, vv, hw, hm, hv, hcopy, cw, cm, cv) = call(
        functools.partial(update_body, plan),
        [shape(*r) for r in results],
        [
            *near,
            *far,
            block_weight,
            block_first,
            block_second,
            member_vectors,
            vectors_first,
            vectors_second,
            head_w,
            head_m,
            head_v,
            biases,
        ],
        [pltpu.VMEM(*r) for r in results]
        + [
            pltpu.VMEM((plan.items // 2, plan.n_mem, plan.groups, LANES), f32),
            pltpu.SemaphoreType.DMA((7 + 8 * plan.quads,)),
        ],
        name="update",
        out_spec=pl.BlockSpec(memory_space=pl.ANY),
    )
    return (
        mean_logits,
        features_grad,
        norm[0, 0],
        bw,
        bm,
        bv,
        bcopy,
        vw,
        vm,
        vv,
        hw[None],
        hm[None],
        hv[None],
        hcopy[None],
        cw,
        cm,
        cv,
    )


def solution(mesh):
    split, whole = P(ALL, None), P()
    heads, biases = P("mem", None, None), P("mem", None)
    return jax.shard_map(
        functools.partial(on_device, mesh),
        mesh=mesh,
        in_specs=(split, P("obj")) + (whole,) * 6 + (heads,) * 3 + (biases,) * 3,
        out_specs=(split, split) + (whole,) * 8 + (heads,) * 4 + (biases,) * 3,
        check_vma=False,
    )
```

```python
import functools
import math

import jax
import jax.numpy as jnp
from jax import lax
from jax.experimental import pallas as pl
from jax.experimental.pallas import tpu as pltpu
from jax.sharding import PartitionSpec as P

STEP = 5
ALL = ("obj", "mem")
LANES = 128
PAD = 16
MIB = 1 << 20

clip_limit = 100.0
beta_one = 0.5
beta_two = 0.5
epsilon = 1e-08
gelu_in = math.sqrt(2.0 / math.pi)
gelu_cube = 0.044715

bf16 = jnp.bfloat16
f32 = jnp.float32
VMEM = pl.BlockSpec(memory_space=pltpu.VMEM)
SMEM = pl.BlockSpec(memory_space=pltpu.SMEM)


def adamw(weight, grad, first, second, rate, decay):
    first_new = beta_one * first + (1.0 - beta_one) * grad
    second_new = beta_two * second + (1.0 - beta_two) * grad * grad
    fix_one = 1.0 / (1.0 - beta_one**STEP)
    fix_two = 1.0 / (1.0 - beta_two**STEP)
    root = lax.rsqrt(second_new * fix_two)
    step_size = first_new * root * (rate * fix_one) / (1.0 + epsilon * root)
    return (weight * (1.0 - rate * decay) - step_size, first_new, second_new)


def dot(a, b, dims=((1,), (0,))):
    return lax.dot_general(a, b, (dims, ((), ())), preferred_element_type=f32)


def call(body, outs, args, scratch=(), name=None, out_spec=VMEM, aliases=None, in_hbm=()):
    specs = [pl.BlockSpec(memory_space=pl.ANY) if i in in_hbm else VMEM for i in range(len(args))]
    return pl.pallas_call(
        body,
        out_shape=outs,
        in_specs=specs,
        out_specs=[out_spec] * len(outs),
        scratch_shapes=list(scratch),
        input_output_aliases=aliases or {},
        compiler_params=pltpu.CompilerParams(vmem_limit_bytes=40 * MIB),
        name=name,
    )(*args)


class Plan:
    def __init__(self, mesh, width, classes, rows):
        self.n_obj, self.n_mem = mesh.shape["obj"], mesh.shape["mem"]
        self.outer = self.n_mem // 2
        self.quads = self.n_obj
        self.shards = 2 * self.quads
        self.width, self.classes, self.rows = width, classes, rows
        self.groups = width // LANES
        self.block_rows = width // self.shards
        self.stacked = self.block_rows * self.groups
        self.items = max(8, self.shards)
        self.bits = [1 << i for i in range(self.outer.bit_length() - 1)]
        self.halving = sorted(range(self.outer), key=lambda k: [k & bit for bit in self.bits])

    def perm(self, move):
        pairs = []
        for obj in range(self.n_obj):
            for mem in range(self.n_mem):
                to_obj, to_mem = move(obj, mem)
                pairs.append((obj * self.n_mem + mem, to_obj * self.n_mem + to_mem))
        return pairs

    def over_core(self, v):
        return lax.ppermute(v, ALL, self.perm(lambda o, m: (o ^ 1, m)))

    def over_plane(self, v, k):
        return lax.ppermute(v, ALL, self.perm(lambda o, m: (o ^ (k >> 1 << 1), m ^ (k & 1))))

    def over_outer(self, v, k):
        return lax.ppermute(v, ALL, self.perm(lambda o, m: (o, m ^ (k << 1))))


def head_body(plan, head_ref, bias_ref, low_ref, held_ref, sem):
    copy = pltpu.make_async_copy(bias_ref, held_ref, sem)
    copy.start()
    low_ref[0 : plan.width, :] = head_ref[...].astype(bf16)
    copy.wait()
    low_ref[plan.width :, :] = jnp.broadcast_to(held_ref[...], (PAD, plan.classes)).astype(bf16)


def low_body(plan, *refs):
    sources, (low_ref, vectors_ref, same_ref, biases_ref, weight_ref, sems) = refs[:6], refs[6:]
    targets = [weight_ref, vectors_ref, same_ref] + [biases_ref.at[i : i + 1] for i in range(3)]
    copies = [
        pltpu.make_async_copy(source, target, sems.at[i])
        for i, (source, target) in enumerate(zip(sources, targets))
    ]
    for copy in copies:
        copy.start()
    for copy in copies:
        copy.wait()
    low_ref[...] = weight_ref[...].astype(bf16)


def forward_body(plan, pieces, *refs):
    feats, (weight_ref, vec_ref) = refs[: len(pieces)], refs[len(pieces) : len(pieces) + 2]
    lifted_ref, mixed_ref, hidden_ref, slope_ref = refs[-4:]
    rows, objs = plan.rows, plan.outer * plan.rows
    outer = place_of()[2]
    tile = 16
    for j in range(2):
        scale_r, scale_s, shift_b = (vec_ref[t, pl.ds(outer * 2 + j, 1), :] for t in range(3))
        first, last = j * objs + pieces[0] * rows, j * objs + (pieces[-1] + 1) * rows
        for k, feat in zip(pieces, feats):
            lifted_ref[j * objs + k * rows : j * objs + (k + 1) * rows, :] = (
                feat[...].astype(f32) * scale_r
            ).astype(bf16)
        mixed_ref[first:last, :] = dot(lifted_ref[first:last, :], weight_ref[...])

        def forward(t, carry):
            at = pl.ds(pl.multiple_of(first + t * tile, tile), tile)
            pre = mixed_ref[at, :] * scale_s + shift_b
            square = pre * pre
            half = 0.5 + 0.5 * jnp.tanh(pre * (gelu_in + (gelu_in * gelu_cube) * square))
            hidden_ref[at, :] = (pre * half).astype(bf16)
            slope_ref[at, :] = half + (half - half * half) * (
                pre * (2.0 * gelu_in + (6.0 * gelu_in * gelu_cube) * square)
            )
            return carry

        steps = (last - first) // tile
        lax.fori_loop(0, steps, forward, 0, unroll=min(steps, 16))


def local_body(plan, *refs):
    n = plan.outer
    feats = refs[:n]
    onehot_ref, weight_ref, vec_ref, own_head, far_head = refs[n : n + 5]
    lifted_ref, mixed_ref, hidden_ref, slope_ref = refs[n + 5 : n + 9]
    send_ref, keep_ref, back_keep, back_send = refs[n + 9 : n + 13]
    dmixed_ref, block_ref, heads_ref, items_ref = refs[n + 13 :]
    rows, width, classes = plan.rows, plan.width, plan.classes
    objs = n * rows
    core, quad, outer, inner = place_of()
    tile = 16

    def member(j):
        return pl.ds(outer * 2 + j, 1)

    items_ref[...] = jnp.zeros_like(items_ref)
    logit_sum = None
    for j in range(2):
        mine = inner == j
        head = jnp.where(mine, own_head[0:width, :], far_head[0:width, :])
        bias = jnp.where(mine, own_head[width : width + 1, :], far_head[width : width + 1, :]).astype(f32)
        hidden = hidden_ref[j * objs : (j + 1) * objs, :]
        logits = dot(hidden, head) + bias
        logit_sum = logits if logit_sum is None else logit_sum + logits
        top = jnp.max(logits, axis=-1, keepdims=True)
        grown = jnp.exp(logits - top)
        soft = grown / jnp.sum(grown, axis=-1, keepdims=True)
        hot = jnp.concatenate(
            [
                onehot_ref[pl.ds(pl.multiple_of(((outer ^ (-p % n)) * 2 + inner) * rows, rows), rows), :]
                for p in range(n)
            ],
            axis=0,
        )
        dlogits = soft - hot
        dlow = dlogits.astype(bf16)
        items_ref[6 + j, 0:1, :] = jnp.sum(dlogits, axis=0, keepdims=True)
        heads_ref[j] = dot(hidden, dlow, ((0,), (0,)))
        mixed_back = dot(dlow, head, ((1,), (1,)))
        block_ref[0:objs, :] = mixed_back
        scale_s = vec_ref[1, member(j), :]

        def backward(t, carry):
            s_sum, b_sum = carry
            at = pl.ds(pl.multiple_of(j * objs + t * tile, tile), tile)
            near = pl.ds(pl.multiple_of(t * tile, tile), tile)
            dpre = block_ref[near, :].astype(bf16).astype(f32) * slope_ref[at, :]
            dmixed_ref[at, :] = (dpre * scale_s).astype(bf16)
            return s_sum + dpre * mixed_ref[at, :], b_sum + dpre

        zero = jnp.zeros((tile, width), f32)
        s_sum, b_sum = lax.fori_loop(0, objs // tile, backward, (zero, zero), unroll=min(objs // tile, 16))
        s_grad = jnp.sum(s_sum, axis=0, keepdims=True)
        b_grad = jnp.sum(b_sum, axis=0, keepdims=True)
        for g in range(plan.groups):
            at = slice(g * LANES, (g + 1) * LANES)
            items_ref[2 + j, g : g + 1, :] = s_grad[:, at]
            items_ref[4 + j, g : g + 1, :] = b_grad[:, at]

    block_ref[...] = dot(dmixed_ref[...], weight_ref[...], ((1,), (1,)))
    r_sums = [jnp.zeros((1, width), f32) for _ in range(2)]
    for spot, k in enumerate(plan.halving):
        p = -k % n
        feat = feats[k][...].astype(f32)
        back = None
        for j in range(2):
            lift_back = block_ref[j * objs + p * rows : j * objs + (p + 1) * rows, :]
            r_sums[j] = r_sums[j] + jnp.sum(lift_back * feat, axis=0, keepdims=True)
            part = lift_back * vec_ref[0, member(j), :]
            back = part if back is None else back + part
        out = back_keep if spot < n // 2 else back_send
        at = slice(spot % (n // 2) * rows, (spot % (n // 2) + 1) * rows)
        out[at, 0:width] = back.astype(out.dtype)
        out[at, width : width + classes] = logit_sum[p * rows : (p + 1) * rows, :].astype(out.dtype)
    for j in range(2):
        for g in range(plan.groups):
            items_ref[j, g : g + 1, :] = r_sums[j][:, g * LANES : (g + 1) * LANES]

    stride = plan.block_rows
    half = width // 2
    for out, side in ((keep_ref, core), (send_ref, 1 - core)):
        part = dot(lifted_ref[:, pl.ds(pl.multiple_of(side * half, half), half)], dmixed_ref[...], ((0,), (0,)))
        for k in range(plan.quads):
            for g in range(plan.groups):
                out[quad ^ k, g * stride : (g + 1) * stride, :] = part[
                    k * stride : (k + 1) * stride, g * LANES : (g + 1) * LANES
                ].astype(out.dtype)
        for k in range(plan.quads):
            shard = side * plan.quads + (quad ^ k)
            at = pl.ds(pl.multiple_of(shard * stride, stride), stride)
            base = plan.stacked
            for j in range(2):
                out[k, base : base + stride, :] = heads_ref[j, at, :].astype(out.dtype)
                base += stride
            out[k, base : base + PAD, :] = items_ref[shard].astype(out.dtype)


def core_body(plan, keep_ref, got_ref, own_ref, *send_refs):
    own_ref[...] = keep_ref[0] + got_ref[0].astype(f32)
    for k in range(1, plan.quads):
        send_refs[k - 1][...] = (keep_ref[k] + got_ref[k].astype(f32)).astype(bf16)


def place_of():
    obj, mem = lax.axis_index("obj"), lax.axis_index("mem")
    return obj % 2, obj // 2 * 2 + mem % 2, mem // 2, mem % 2


def two_parts(v):
    high = v.astype(bf16).astype(f32)
    return high, v - high


def plane_body(plan, own_ref, *refs):
    got, (send_ref, block_ref, head_ref) = refs[: plan.quads - 1], refs[plan.quads - 1 :]
    total = own_ref[...]
    for r in got:
        total = total + r[...].astype(f32)
    base = plan.stacked
    block_ref[0:base, :] = total[0:base, :]
    send_ref[0:base, :] = total[0:base, :].astype(bf16)
    heads = total[base : base + 2 * plan.block_rows, :]
    head_ref[...] = heads
    squares = jnp.sum(jnp.sum(heads * heads, axis=1, keepdims=True), axis=0, keepdims=True)
    high, low = two_parts(jnp.broadcast_to(squares, (PAD, LANES)))
    items = total[base + 2 * plan.block_rows :, :]
    row = lax.broadcasted_iota(jnp.int32, (PAD, LANES), 0)
    extra = jnp.where(row < plan.groups, items, jnp.where(row == plan.groups, high, low))
    block_ref[base : base + PAD, :] = extra
    send_ref[base : base + PAD, :] = extra.astype(bf16)


def outer_body(plan, block_ref, head_ref, *refs):
    n = plan.outer
    got, (same_ref, flip_ref) = refs[: n - 1], refs[n - 1 :]
    inner = place_of()[3]
    base, stride, groups = plan.stacked, plan.block_rows, plan.groups
    total = block_ref[0:base, :]
    extras = [block_ref[base : base + PAD, :].astype(bf16).astype(f32)]
    for r in got:
        total = total + r[0:base, :].astype(f32)
        extras.append(r[base : base + PAD, :].astype(f32))
    row = lax.broadcasted_iota(jnp.int32, (PAD, LANES), 0)
    head_squares = jnp.zeros((1, LANES), f32)
    item_squares = jnp.zeros((PAD, LANES), f32)
    for extra in extras:
        head_squares = head_squares + extra[groups : groups + 1, :] + extra[groups + 1 : groups + 2, :]
        item_squares = item_squares + jnp.where(row < groups, extra * extra, 0.0)
    squares = (
        jnp.sum(jnp.sum(total * total, axis=1, keepdims=True), axis=0, keepdims=True)
        + jnp.sum(jnp.sum(item_squares, axis=1, keepdims=True), axis=0, keepdims=True)
        + head_squares
    )
    high, low = two_parts(jnp.broadcast_to(squares, (PAD, LANES)))
    items = jnp.concatenate([extra[0:groups, :] for extra in extras], axis=0).astype(bf16)
    sums = jnp.where(row == 0, high, low).astype(bf16)
    block = total.astype(bf16)
    for out, member in ((same_ref, inner), (flip_ref, 1 - inner)):
        at = pl.ds(pl.multiple_of(member * stride, stride), stride)
        out[0:base, :] = block
        out[base : base + groups * n, :] = items
        spot = base + groups * n
        out[spot : spot + stride, :] = head_ref[at, :].astype(bf16)
        out[spot + stride : spot + stride + PAD, :] = sums


def half_body(plan, had_ref, got_ref, keep_ref, send_ref):
    half = keep_ref.shape[0]
    keep_ref[...] = had_ref[0:half, :] + got_ref[0:half, :].astype(f32)
    send_ref[...] = (had_ref[half : 2 * half, :] + got_ref[half : 2 * half, :].astype(f32)).astype(bf16)


def back_body(plan, had_ref, got_ref, feat_ref, mean_ref):
    total = had_ref[...] + got_ref[...].astype(f32)
    feat_ref[...] = total[:, 0 : plan.width]
    mean_ref[...] = total[:, plan.width :] / plan.n_mem


def update_body(plan, *refs):
    chunks = refs[: plan.shards]
    states = refs[plan.shards : plan.shards + 10]
    outs = refs[plan.shards + 10 : plan.shards + 25]
    held, items_ref, sems = refs[plan.shards + 25 : -2], refs[-2], refs[-1]
    bw, bm, bv, vw, vm, vv, hw, hm, hv, cs = states
    norm_out, vec_outs, bias_outs, block_outs, head_outs = (
        outs[0],
        outs[5:8],
        outs[12:15],
        outs[1:5],
        outs[8:12],
    )
    norm_ref, vec_refs, bias_refs, block_refs, head_refs = (
        held[0],
        held[5:8],
        held[12:15],
        held[1:5],
        held[8:12],
    )
    core, quad, outer, inner = place_of()
    n, groups, stride, base = plan.outer, plan.groups, plan.block_rows, plan.stacked
    spot = base + groups * n
    copies = []

    def send(source, target):
        copies.append(pltpu.make_async_copy(source, target, sems.at[len(copies)]))
        copies[-1].start()

    squares = jnp.zeros((1, LANES), f32)
    for chunk in chunks:
        sums = chunk[spot + stride : spot + stride + PAD, :].astype(f32)
        squares = squares + sums[0:1, :] + sums[1:2, :]
    norm = jnp.sqrt(squares)
    norm_ref[...] = norm
    factor = clip_limit / jnp.maximum(norm, clip_limit)
    send(norm_ref, norm_out)

    def shard_of(i):
        side, k = divmod(i, plan.quads)
        return (core ^ side) * plan.quads + (quad ^ k)

    for i, chunk in enumerate(chunks):
        at = pl.ds(pl.multiple_of(shard_of(i) * stride, stride), stride)
        for g in range(groups):
            lanes = slice(g * LANES, (g + 1) * LANES)
            grad = chunk[g * stride : (g + 1) * stride, :].astype(f32) * factor
            new = adamw(bw[at, lanes], grad, bm[at, lanes], bv[at, lanes], 0.02, 0.01)
            for ref, v in zip(block_refs, new + (new[0],)):
                ref[at, lanes] = v.astype(ref.dtype)
        grad = chunk[spot : spot + stride, :].astype(f32) * factor
        new = adamw(hw[at, :], grad, hm[at, :], hv[at, :], 0.02, 0.01)
        for ref, v in zip(head_refs, new + (new[0],)):
            ref[at, :] = v.astype(ref.dtype)
        if i < 2:
            for source, target in zip(block_refs + head_refs, block_outs + head_outs):
                send(source.at[at], target.at[at])
        elif i % 2:
            both = pl.ds(pl.multiple_of(shard_of(i) // 2 * (2 * stride), 2 * stride), 2 * stride)
            for source, target in zip(block_refs + head_refs, block_outs + head_outs):
                send(source.at[both], target.at[both])
    for i, chunk in enumerate(chunks):
        shard = shard_of(i)
        items = chunk[base : base + groups * n, :].astype(f32)
        for z in range(n):
            items_ref[shard // 2, (outer ^ z) * 2 + shard % 2] = items[z * groups : (z + 1) * groups, :]
    wide = jnp.concatenate([factor] * groups, axis=1)
    for t in range(3):
        grad = jnp.concatenate([items_ref[t, :, g, :] for g in range(groups)], axis=1) * wide
        for ref, v in zip(vec_refs, adamw(vw[t], grad, vm[t], vv[t], 0.5, 0.0)):
            ref[t] = v
    grad = items_ref[3, outer * 2 + inner, 0:1, :] * factor
    for ref, v in zip(bias_refs, adamw(cs[0:1, :], grad, cs[1:2, :], cs[2:3, :], 0.1, 0.0)):
        ref[...] = v
    for source, target in zip(vec_refs + bias_refs, vec_outs + bias_outs):
        send(source, target)

    for copy in copies:
        copy.wait()


def on_device(
    mesh,
    features,
    labels,
    block_weight,
    block_first,
    block_second,
    member_vectors,
    vectors_first,
    vectors_second,
    head_weight,
    head_first,
    head_second,
    head_bias,
    bias_first,
    bias_second,
):
    rows, width = features.shape
    classes = head_weight.shape[-1]
    plan = Plan(mesh, width, classes, rows)
    n, quads, stride = plan.outer, plan.quads, plan.block_rows
    shape = jax.ShapeDtypeStruct

    far_feats = [plan.over_outer(features, k) for k in range(n - 1, 0, -1)][::-1]
    (own_head,) = call(
        functools.partial(head_body, plan),
        [shape((width + PAD, classes), bf16)],
        [head_weight[0], head_bias],
        [pltpu.VMEM(head_bias.shape, f32), pltpu.SemaphoreType.DMA],
        name="head_low",
        in_hbm=(1,),
    )
    far_head = plan.over_plane(own_head, 1)
    weight_low, vectors, late, biases = call(
        functools.partial(low_body, plan),
        [
            shape((width, width), bf16),
            shape(member_vectors.shape, f32),
            shape((rows, width), bf16),
            shape((3, classes), f32),
        ],
        [
            pltpu.with_memory_space_constraint(v, pltpu.HBM)
            for v in (block_weight, member_vectors, features, head_bias, bias_first, bias_second)
        ],
        [pltpu.VMEM((width, width), f32), pltpu.SemaphoreType.DMA((6,))],
        name="weight_low",
        in_hbm=range(6),
    )
    onehot = (
        jnp.arange(classes, dtype=jnp.int32)[None, :] == labels[:, None]
    ).astype(f32)

    objs = n * rows
    total = plan.stacked + 2 * stride + PAD
    back = width + classes
    done = ()
    for pieces in (range(n),):
        done = call(
            functools.partial(forward_body, plan, pieces),
            [shape((2 * objs, width), dtype) for dtype in (bf16, f32, bf16, f32)],
            [([late] + far_feats)[-k] for k in pieces] + [weight_low, vectors, *done],
            name="forward",
            aliases={3 + i: i for i in range(len(done))},
        )
    outs = call(
        functools.partial(local_body, plan),
        [
            shape((quads, total, LANES), bf16),
            shape((quads, total, LANES), f32),
            shape((objs // 2, back), f32),
            shape((objs // 2, back), bf16),
        ],
        [features, *far_feats, onehot, weight_low, vectors, own_head, far_head, *done],
        [
            pltpu.VMEM((2 * objs, width), bf16),
            pltpu.VMEM((2 * objs, width), f32),
            pltpu.VMEM((2, width, classes), f32),
            pltpu.VMEM((plan.items, PAD, LANES), f32),
        ],
        name="local",
    )
    send, keep, back_keep, back_send = outs

    got = plan.over_core(send)
    own, *sends = call(
        functools.partial(core_body, plan),
        [shape((total, LANES), f32)] + [shape((total, LANES), bf16)] * (quads - 1),
        [keep, got],
        name="core_sum",
    )
    got = [plan.over_plane(v, k + 1) for k, v in enumerate(sends)]
    for bit in plan.bits[:-1]:
        half = back_keep.shape[0] // 2
        back_keep, back_send = call(
            functools.partial(half_body, plan),
            [shape((half, back), f32), shape((half, back), bf16)],
            [back_keep, plan.over_outer(back_send, bit)],
            name="back_half",
        )
    own, back_send, back_keep = lax.optimization_barrier((own, back_send, back_keep))
    send, block, heads = call(
        functools.partial(plane_body, plan),
        [
            shape((plan.stacked + PAD, LANES), bf16),
            shape((plan.stacked + PAD, LANES), f32),
            shape((2 * stride, LANES), f32),
        ],
        [own, *got],
        name="plane_sum",
    )
    got = [plan.over_outer(send, k) for k in range(1, n)]
    features_grad, mean_logits = call(
        functools.partial(back_body, plan),
        [shape((rows, width), f32), shape((rows, classes), f32)],
        [back_keep, plan.over_outer(back_send, plan.bits[-1])],
        name="back_sum",
    )
    got, features_grad, mean_logits = lax.optimization_barrier((got, features_grad, mean_logits))
    last = plan.stacked + plan.groups * n + stride + PAD
    same, flip = call(
        functools.partial(outer_body, plan),
        [shape((last, LANES), bf16)] * 2,
        [block, heads, *got],
        name="outer_sum",
    )
    near = [same] + [plan.over_plane(flip if k & 1 else same, k) for k in range(1, quads)]
    far = [plan.over_core(v) for v in near]

    like = lambda v, dtype=f32: (v.shape, dtype)
    head_w, head_m, head_v = head_weight[0], head_first[0], head_second[0]
    results = (
        [((1, LANES), f32)]
        + [like(block_weight)] * 3
        + [like(block_weight, bf16)]
        + [like(member_vectors)] * 3
        + [like(head_w)] * 3
        + [like(head_w, bf16)]
        + [like(head_bias)] * 3
    )
    (norm, bw, bm, bv, bcopy, vw, vm, vv, hw, hm, hv, hcopy, cw, cm, cv) = call(
        functools.partial(update_body, plan),
        [shape(*r) for r in results],
        [
            *near,
            *far,
            block_weight,
            block_first,
            block_second,
            member_vectors,
            vectors_first,
            vectors_second,
            head_w,
            head_m,
            head_v,
            biases,
        ],
        [pltpu.VMEM(*r) for r in results]
        + [
            pltpu.VMEM((plan.items // 2, plan.n_mem, plan.groups, LANES), f32),
            pltpu.SemaphoreType.DMA((15 + 8 * plan.quads,)),
        ],
        name="update",
        out_spec=pl.BlockSpec(memory_space=pl.ANY),
    )
    return (
        mean_logits,
        features_grad,
        norm[0, 0],
        bw,
        bm,
        bv,
        bcopy,
        vw,
        vm,
        vv,
        hw[None],
        hm[None],
        hv[None],
        hcopy[None],
        cw,
        cm,
        cv,
    )


def solution(mesh):
    split, whole = P(ALL, None), P()
    heads, biases = P("mem", None, None), P("mem", None)
    return jax.shard_map(
        functools.partial(on_device, mesh),
        mesh=mesh,
        in_specs=(split, P("obj")) + (whole,) * 6 + (heads,) * 3 + (biases,) * 3,
        out_specs=(split, split) + (whole,) * 8 + (heads,) * 4 + (biases,) * 3,
        check_vma=False,
    )
```

```python
import functools
import math

import jax
import jax.numpy as jnp
from jax import lax
from jax.experimental import pallas as pl
from jax.experimental.pallas import tpu as pltpu
from jax.sharding import PartitionSpec as P

STEP = 5
ALL = ("obj", "mem")
LANES = 128
PAD = 16
MIB = 1 << 20

clip_limit = 100.0
beta_one = 0.5
beta_two = 0.5
epsilon = 1e-08
gelu_in = math.sqrt(2.0 / math.pi)
gelu_cube = 0.044715

bf16 = jnp.bfloat16
f32 = jnp.float32
VMEM = pl.BlockSpec(memory_space=pltpu.VMEM)
SMEM = pl.BlockSpec(memory_space=pltpu.SMEM)


def adamw(weight, grad, first, second, rate, decay):
    first_new = beta_one * first + (1.0 - beta_one) * grad
    second_new = beta_two * second + (1.0 - beta_two) * grad * grad
    fix_one = 1.0 / (1.0 - beta_one**STEP)
    fix_two = 1.0 / (1.0 - beta_two**STEP)
    root = lax.rsqrt(second_new * fix_two)
    step_size = first_new * root * (rate * fix_one) / (1.0 + epsilon * root)
    return (weight * (1.0 - rate * decay) - step_size, first_new, second_new)


def dot(a, b, dims=((1,), (0,))):
    return lax.dot_general(a, b, (dims, ((), ())), preferred_element_type=f32)


def call(body, outs, args, scratch=(), name=None, out_spec=VMEM, aliases=None, in_hbm=()):
    specs = [pl.BlockSpec(memory_space=pl.ANY) if i in in_hbm else VMEM for i in range(len(args))]
    return pl.pallas_call(
        body,
        out_shape=outs,
        in_specs=specs,
        out_specs=[out_spec] * len(outs),
        scratch_shapes=list(scratch),
        input_output_aliases=aliases or {},
        compiler_params=pltpu.CompilerParams(vmem_limit_bytes=40 * MIB),
        name=name,
    )(*args)


class Plan:
    def __init__(self, mesh, width, classes, rows):
        self.n_obj, self.n_mem = mesh.shape["obj"], mesh.shape["mem"]
        self.outer = self.n_mem // 2
        self.quads = self.n_obj
        self.shards = 2 * self.quads
        self.width, self.classes, self.rows = width, classes, rows
        self.groups = width // LANES
        self.block_rows = width // self.shards
        self.stacked = self.block_rows * self.groups
        self.items = max(8, self.shards)
        self.bits = [1 << i for i in range(self.outer.bit_length() - 1)]
        self.halving = sorted(range(self.outer), key=lambda k: [k & bit for bit in self.bits])

    def perm(self, move):
        pairs = []
        for obj in range(self.n_obj):
            for mem in range(self.n_mem):
                to_obj, to_mem = move(obj, mem)
                pairs.append((obj * self.n_mem + mem, to_obj * self.n_mem + to_mem))
        return pairs

    def over_core(self, v):
        return lax.ppermute(v, ALL, self.perm(lambda o, m: (o ^ 1, m)))

    def over_plane(self, v, k):
        return lax.ppermute(v, ALL, self.perm(lambda o, m: (o ^ (k >> 1 << 1), m ^ (k & 1))))

    def over_outer(self, v, k):
        return lax.ppermute(v, ALL, self.perm(lambda o, m: (o, m ^ (k << 1))))


def head_body(plan, head_ref, bias_ref, low_ref, held_ref, sem):
    copy = pltpu.make_async_copy(bias_ref, held_ref, sem)
    copy.start()
    low_ref[0 : plan.width, :] = head_ref[...].astype(bf16)
    copy.wait()
    low_ref[plan.width :, :] = jnp.broadcast_to(held_ref[...], (PAD, plan.classes)).astype(bf16)


def low_body(plan, weight_ref, bias_ref, first_ref, second_ref, low_ref, biases_ref):
    low_ref[...] = weight_ref[...].astype(bf16)
    for i, ref in enumerate((bias_ref, first_ref, second_ref)):
        biases_ref[i : i + 1, :] = ref[...]


def forward_body(plan, pieces, *refs):
    feats, (weight_ref, vec_ref) = refs[: len(pieces)], refs[len(pieces) : len(pieces) + 2]
    lifted_ref, mixed_ref, hidden_ref, slope_ref = refs[-4:]
    rows, objs = plan.rows, plan.outer * plan.rows
    outer = place_of()[2]
    tile = 16
    for j in range(2):
        scale_r, scale_s, shift_b = (vec_ref[t, pl.ds(outer * 2 + j, 1), :] for t in range(3))
        first, last = j * objs + pieces[0] * rows, j * objs + (pieces[-1] + 1) * rows
        for k, feat in zip(pieces, feats):
            lifted_ref[j * objs + k * rows : j * objs + (k + 1) * rows, :] = (
                feat[...].astype(f32) * scale_r
            ).astype(bf16)
        mixed_ref[first:last, :] = dot(lifted_ref[first:last, :], weight_ref[...])

        def forward(t, carry):
            at = pl.ds(pl.multiple_of(first + t * tile, tile), tile)
            pre = mixed_ref[at, :] * scale_s + shift_b
            square = pre * pre
            half = 0.5 + 0.5 * jnp.tanh(pre * (gelu_in + (gelu_in * gelu_cube) * square))
            hidden_ref[at, :] = (pre * half).astype(bf16)
            slope_ref[at, :] = half + (half - half * half) * (
                pre * (2.0 * gelu_in + (6.0 * gelu_in * gelu_cube) * square)
            )
            return carry

        steps = (last - first) // tile
        lax.fori_loop(0, steps, forward, 0, unroll=min(steps, 16))


def local_body(plan, *refs):
    n = plan.outer
    feats = refs[:n]
    onehot_ref, weight_ref, vec_ref, own_head, far_head = refs[n : n + 5]
    lifted_ref, mixed_ref, hidden_ref, slope_ref = refs[n + 5 : n + 9]
    send_ref, keep_ref, back_keep, back_send = refs[n + 9 : n + 13]
    dmixed_ref, block_ref, heads_ref, items_ref = refs[n + 13 :]
    rows, width, classes = plan.rows, plan.width, plan.classes
    objs = n * rows
    core, quad, outer, inner = place_of()
    tile = 16

    def member(j):
        return pl.ds(outer * 2 + j, 1)

    items_ref[...] = jnp.zeros_like(items_ref)
    logit_sum = None
    for j in range(2):
        mine = inner == j
        head = jnp.where(mine, own_head[0:width, :], far_head[0:width, :])
        bias = jnp.where(mine, own_head[width : width + 1, :], far_head[width : width + 1, :]).astype(f32)
        hidden = hidden_ref[j * objs : (j + 1) * objs, :]
        logits = dot(hidden, head) + bias
        logit_sum = logits if logit_sum is None else logit_sum + logits
        top = jnp.max(logits, axis=-1, keepdims=True)
        grown = jnp.exp(logits - top)
        soft = grown / jnp.sum(grown, axis=-1, keepdims=True)
        hot = jnp.concatenate(
            [
                onehot_ref[pl.ds(pl.multiple_of(((outer ^ (-p % n)) * 2 + inner) * rows, rows), rows), :]
                for p in range(n)
            ],
            axis=0,
        )
        dlogits = soft - hot
        dlow = dlogits.astype(bf16)
        items_ref[6 + j, 0:1, :] = jnp.sum(dlogits, axis=0, keepdims=True)
        heads_ref[j] = dot(hidden, dlow, ((0,), (0,)))
        mixed_back = dot(dlow, head, ((1,), (1,)))
        block_ref[0:objs, :] = mixed_back
        scale_s = vec_ref[1, member(j), :]

        def backward(t, carry):
            s_sum, b_sum = carry
            at = pl.ds(pl.multiple_of(j * objs + t * tile, tile), tile)
            near = pl.ds(pl.multiple_of(t * tile, tile), tile)
            dpre = block_ref[near, :].astype(bf16).astype(f32) * slope_ref[at, :]
            dmixed_ref[at, :] = (dpre * scale_s).astype(bf16)
            return s_sum + dpre * mixed_ref[at, :], b_sum + dpre

        zero = jnp.zeros((tile, width), f32)
        s_sum, b_sum = lax.fori_loop(0, objs // tile, backward, (zero, zero), unroll=min(objs // tile, 16))
        s_grad = jnp.sum(s_sum, axis=0, keepdims=True)
        b_grad = jnp.sum(b_sum, axis=0, keepdims=True)
        for g in range(plan.groups):
            at = slice(g * LANES, (g + 1) * LANES)
            items_ref[2 + j, g : g + 1, :] = s_grad[:, at]
            items_ref[4 + j, g : g + 1, :] = b_grad[:, at]

    block_ref[...] = dot(dmixed_ref[...], weight_ref[...], ((1,), (1,)))
    r_sums = [jnp.zeros((1, width), f32) for _ in range(2)]
    for spot, k in enumerate(plan.halving):
        p = -k % n
        feat = feats[k][...].astype(f32)
        back = None
        for j in range(2):
            lift_back = block_ref[j * objs + p * rows : j * objs + (p + 1) * rows, :]
            r_sums[j] = r_sums[j] + jnp.sum(lift_back * feat, axis=0, keepdims=True)
            part = lift_back * vec_ref[0, member(j), :]
            back = part if back is None else back + part
        out = back_keep if spot < n // 2 else back_send
        at = slice(spot % (n // 2) * rows, (spot % (n // 2) + 1) * rows)
        out[at, 0:width] = back.astype(out.dtype)
        out[at, width : width + classes] = logit_sum[p * rows : (p + 1) * rows, :].astype(out.dtype)
    for j in range(2):
        for g in range(plan.groups):
            items_ref[j, g : g + 1, :] = r_sums[j][:, g * LANES : (g + 1) * LANES]

    stride = plan.block_rows
    half = width // 2
    for out, side in ((keep_ref, core), (send_ref, 1 - core)):
        part = dot(lifted_ref[:, pl.ds(pl.multiple_of(side * half, half), half)], dmixed_ref[...], ((0,), (0,)))
        for k in range(plan.quads):
            for g in range(plan.groups):
                out[quad ^ k, g * stride : (g + 1) * stride, :] = part[
                    k * stride : (k + 1) * stride, g * LANES : (g + 1) * LANES
                ].astype(out.dtype)
        for k in range(plan.quads):
            shard = side * plan.quads + (quad ^ k)
            at = pl.ds(pl.multiple_of(shard * stride, stride), stride)
            base = plan.stacked
            for j in range(2):
                out[k, base : base + stride, :] = heads_ref[j, at, :].astype(out.dtype)
                base += stride
            out[k, base : base + PAD, :] = items_ref[shard].astype(out.dtype)


def core_body(plan, keep_ref, got_ref, own_ref, *send_refs):
    own_ref[...] = keep_ref[0].astype(f32) + got_ref[0].astype(f32)
    for k in range(1, plan.quads):
        send_refs[k - 1][...] = (keep_ref[k].astype(f32) + got_ref[k].astype(f32)).astype(bf16)


def place_of():
    obj, mem = lax.axis_index("obj"), lax.axis_index("mem")
    return obj % 2, obj // 2 * 2 + mem % 2, mem // 2, mem % 2


def two_parts(v):
    high = v.astype(bf16).astype(f32)
    return high, v - high


def plane_body(plan, own_ref, *refs):
    got, (send_ref, block_ref, head_ref) = refs[: plan.quads - 1], refs[plan.quads - 1 :]
    total = own_ref[...]
    for r in got:
        total = total + r[...].astype(f32)
    base = plan.stacked
    block_ref[0:base, :] = total[0:base, :]
    send_ref[0:base, :] = total[0:base, :].astype(bf16)
    heads = total[base : base + 2 * plan.block_rows, :]
    head_ref[...] = heads
    squares = jnp.sum(jnp.sum(heads * heads, axis=1, keepdims=True), axis=0, keepdims=True)
    high, low = two_parts(jnp.broadcast_to(squares, (PAD, LANES)))
    items = total[base + 2 * plan.block_rows :, :]
    row = lax.broadcasted_iota(jnp.int32, (PAD, LANES), 0)
    extra = jnp.where(row < plan.groups, items, jnp.where(row == plan.groups, high, low))
    block_ref[base : base + PAD, :] = extra
    send_ref[base : base + PAD, :] = extra.astype(bf16)


def outer_body(plan, block_ref, head_ref, *refs):
    n = plan.outer
    got, (same_ref, flip_ref) = refs[: n - 1], refs[n - 1 :]
    inner = place_of()[3]
    base, stride, groups = plan.stacked, plan.block_rows, plan.groups
    total = block_ref[0:base, :]
    extras = [block_ref[base : base + PAD, :].astype(bf16).astype(f32)]
    for r in got:
        total = total + r[0:base, :].astype(f32)
        extras.append(r[base : base + PAD, :].astype(f32))
    row = lax.broadcasted_iota(jnp.int32, (PAD, LANES), 0)
    head_squares = jnp.zeros((1, LANES), f32)
    item_squares = jnp.zeros((PAD, LANES), f32)
    for extra in extras:
        head_squares = head_squares + extra[groups : groups + 1, :] + extra[groups + 1 : groups + 2, :]
        item_squares = item_squares + jnp.where(row < groups, extra * extra, 0.0)
    squares = (
        jnp.sum(jnp.sum(total * total, axis=1, keepdims=True), axis=0, keepdims=True)
        + jnp.sum(jnp.sum(item_squares, axis=1, keepdims=True), axis=0, keepdims=True)
        + head_squares
    )
    high, low = two_parts(jnp.broadcast_to(squares, (PAD, LANES)))
    items = jnp.concatenate([extra[0:groups, :] for extra in extras], axis=0).astype(bf16)
    sums = jnp.where(row == 0, high, low).astype(bf16)
    block = total.astype(bf16)
    for out, member in ((same_ref, inner), (flip_ref, 1 - inner)):
        at = pl.ds(pl.multiple_of(member * stride, stride), stride)
        out[0:base, :] = block
        out[base : base + groups * n, :] = items
        spot = base + groups * n
        out[spot : spot + stride, :] = head_ref[at, :].astype(bf16)
        out[spot + stride : spot + stride + PAD, :] = sums


def half_body(plan, had_ref, got_ref, keep_ref, send_ref):
    half = keep_ref.shape[0]
    keep_ref[...] = had_ref[0:half, :] + got_ref[0:half, :].astype(f32)
    send_ref[...] = (had_ref[half : 2 * half, :] + got_ref[half : 2 * half, :].astype(f32)).astype(bf16)


def back_body(plan, had_ref, got_ref, feat_ref, mean_ref):
    total = had_ref[...] + got_ref[...].astype(f32)
    feat_ref[...] = total[:, 0 : plan.width]
    mean_ref[...] = total[:, plan.width :] / plan.n_mem


def update_body(plan, *refs):
    chunks = refs[: plan.shards]
    states = refs[plan.shards : plan.shards + 10]
    outs = refs[plan.shards + 10 : plan.shards + 25]
    held, items_ref, sems = refs[plan.shards + 25 : -2], refs[-2], refs[-1]
    bw, bm, bv, vw, vm, vv, hw, hm, hv, cs = states
    norm_out, vec_outs, bias_outs, block_outs, head_outs = (
        outs[0],
        outs[5:8],
        outs[12:15],
        outs[1:5],
        outs[8:12],
    )
    norm_ref, vec_refs, bias_refs, block_refs, head_refs = (
        held[0],
        held[5:8],
        held[12:15],
        held[1:5],
        held[8:12],
    )
    core, quad, outer, inner = place_of()
    n, groups, stride, base = plan.outer, plan.groups, plan.block_rows, plan.stacked
    spot = base + groups * n
    copies = []

    def send(source, target):
        copies.append(pltpu.make_async_copy(source, target, sems.at[len(copies)]))
        copies[-1].start()

    squares = jnp.zeros((1, LANES), f32)
    for chunk in chunks:
        sums = chunk[spot + stride : spot + stride + PAD, :].astype(f32)
        squares = squares + sums[0:1, :] + sums[1:2, :]
    norm = jnp.sqrt(squares)
    norm_ref[...] = norm
    factor = clip_limit / jnp.maximum(norm, clip_limit)
    send(norm_ref, norm_out)

    def shard_of(i):
        side, k = divmod(i, plan.quads)
        return (core ^ side) * plan.quads + (quad ^ k)

    for i, chunk in enumerate(chunks):
        at = pl.ds(pl.multiple_of(shard_of(i) * stride, stride), stride)
        for g in range(groups):
            lanes = slice(g * LANES, (g + 1) * LANES)
            grad = chunk[g * stride : (g + 1) * stride, :].astype(f32) * factor
            new = adamw(bw[at, lanes], grad, bm[at, lanes], bv[at, lanes], 0.02, 0.01)
            for ref, v in zip(block_refs, new + (new[0],)):
                ref[at, lanes] = v.astype(ref.dtype)
        grad = chunk[spot : spot + stride, :].astype(f32) * factor
        new = adamw(hw[at, :], grad, hm[at, :], hv[at, :], 0.02, 0.01)
        for ref, v in zip(head_refs, new + (new[0],)):
            ref[at, :] = v.astype(ref.dtype)
        if i < 2:
            for source, target in zip(block_refs + head_refs, block_outs + head_outs):
                send(source.at[at], target.at[at])
        elif i % 2:
            both = pl.ds(pl.multiple_of(shard_of(i) // 2 * (2 * stride), 2 * stride), 2 * stride)
            for source, target in zip(block_refs + head_refs, block_outs + head_outs):
                send(source.at[both], target.at[both])
    for i, chunk in enumerate(chunks):
        shard = shard_of(i)
        items = chunk[base : base + groups * n, :].astype(f32)
        for z in range(n):
            items_ref[shard // 2, (outer ^ z) * 2 + shard % 2] = items[z * groups : (z + 1) * groups, :]
    wide = jnp.concatenate([factor] * groups, axis=1)
    for t in range(3):
        grad = jnp.concatenate([items_ref[t, :, g, :] for g in range(groups)], axis=1) * wide
        for ref, v in zip(vec_refs, adamw(vw[t], grad, vm[t], vv[t], 0.5, 0.0)):
            ref[t] = v
    grad = items_ref[3, outer * 2 + inner, 0:1, :] * factor
    for ref, v in zip(bias_refs, adamw(cs[0:1, :], grad, cs[1:2, :], cs[2:3, :], 0.1, 0.0)):
        ref[...] = v
    for source, target in zip(vec_refs + bias_refs, vec_outs + bias_outs):
        send(source, target)

    for copy in copies:
        copy.wait()


def on_device(
    mesh,
    features,
    labels,
    block_weight,
    block_first,
    block_second,
    member_vectors,
    vectors_first,
    vectors_second,
    head_weight,
    head_first,
    head_second,
    head_bias,
    bias_first,
    bias_second,
):
    rows, width = features.shape
    classes = head_weight.shape[-1]
    plan = Plan(mesh, width, classes, rows)
    n, quads, stride = plan.outer, plan.quads, plan.block_rows
    shape = jax.ShapeDtypeStruct

    far_feats = [plan.over_outer(features, k) for k in range(n - 1, 0, -1)][::-1]
    (own_head,) = call(
        functools.partial(head_body, plan),
        [shape((width + PAD, classes), bf16)],
        [head_weight[0], head_bias],
        [pltpu.VMEM(head_bias.shape, f32), pltpu.SemaphoreType.DMA],
        name="head_low",
        in_hbm=(1,),
    )
    far_head = plan.over_plane(own_head, 1)
    weight_low, biases = call(
        functools.partial(low_body, plan),
        [shape((width, width), bf16), shape((3, classes), f32)],
        [block_weight, head_bias, bias_first, bias_second],
        name="weight_low",
    )
    onehot = (
        jnp.arange(classes, dtype=jnp.int32)[None, :] == labels[:, None]
    ).astype(f32)

    objs = n * rows
    total = plan.stacked + 2 * stride + PAD
    back = width + classes
    done = ()
    for pieces in (range(n),):
        done = call(
            functools.partial(forward_body, plan, pieces),
            [shape((2 * objs, width), dtype) for dtype in (bf16, f32, bf16, f32)],
            [([features] + far_feats)[-k] for k in pieces] + [weight_low, member_vectors, *done],
            name="forward",
            aliases={3 + i: i for i in range(len(done))},
        )
    outs = call(
        functools.partial(local_body, plan),
        [
            shape((quads, total, LANES), bf16),
            shape((quads, total, LANES), bf16),
            shape((objs // 2, back), f32),
            shape((objs // 2, back), bf16),
        ],
        [features, *far_feats, onehot, weight_low, member_vectors, own_head, far_head, *done],
        [
            pltpu.VMEM((2 * objs, width), bf16),
            pltpu.VMEM((2 * objs, width), f32),
            pltpu.VMEM((2, width, classes), f32),
            pltpu.VMEM((plan.items, PAD, LANES), f32),
        ],
        name="local",
    )
    send, keep, back_keep, back_send = outs

    got = plan.over_core(send)
    own, *sends = call(
        functools.partial(core_body, plan),
        [shape((total, LANES), f32)] + [shape((total, LANES), bf16)] * (quads - 1),
        [keep, got],
        name="core_sum",
    )
    got = [plan.over_plane(v, k + 1) for k, v in enumerate(sends)]
    for bit in plan.bits[:-1]:
        half = back_keep.shape[0] // 2
        back_keep, back_send = call(
            functools.partial(half_body, plan),
            [shape((half, back), f32), shape((half, back), bf16)],
            [back_keep, plan.over_outer(back_send, bit)],
            name="back_half",
        )
    own, back_send, back_keep = lax.optimization_barrier((own, back_send, back_keep))
    send, block, heads = call(
        functools.partial(plane_body, plan),
        [
            shape((plan.stacked + PAD, LANES), bf16),
            shape((plan.stacked + PAD, LANES), f32),
            shape((2 * stride, LANES), f32),
        ],
        [own, *got],
        name="plane_sum",
    )
    got = [plan.over_outer(send, k) for k in range(1, n)]
    features_grad, mean_logits = call(
        functools.partial(back_body, plan),
        [shape((rows, width), f32), shape((rows, classes), f32)],
        [back_keep, plan.over_outer(back_send, plan.bits[-1])],
        name="back_sum",
    )
    got, features_grad, mean_logits = lax.optimization_barrier((got, features_grad, mean_logits))
    last = plan.stacked + plan.groups * n + stride + PAD
    same, flip = call(
        functools.partial(outer_body, plan),
        [shape((last, LANES), bf16)] * 2,
        [block, heads, *got],
        name="outer_sum",
    )
    near = [same] + [plan.over_plane(flip if k & 1 else same, k) for k in range(1, quads)]
    far = [plan.over_core(v) for v in near]

    like = lambda v, dtype=f32: (v.shape, dtype)
    head_w, head_m, head_v = head_weight[0], head_first[0], head_second[0]
    results = (
        [((1, LANES), f32)]
        + [like(block_weight)] * 3
        + [like(block_weight, bf16)]
        + [like(member_vectors)] * 3
        + [like(head_w)] * 3
        + [like(head_w, bf16)]
        + [like(head_bias)] * 3
    )
    (norm, bw, bm, bv, bcopy, vw, vm, vv, hw, hm, hv, hcopy, cw, cm, cv) = call(
        functools.partial(update_body, plan),
        [shape(*r) for r in results],
        [
            *near,
            *far,
            block_weight,
            block_first,
            block_second,
            member_vectors,
            vectors_first,
            vectors_second,
            head_w,
            head_m,
            head_v,
            biases,
        ],
        [pltpu.VMEM(*r) for r in results]
        + [
            pltpu.VMEM((plan.items // 2, plan.n_mem, plan.groups, LANES), f32),
            pltpu.SemaphoreType.DMA((15 + 8 * plan.quads,)),
        ],
        name="update",
        out_spec=pl.BlockSpec(memory_space=pl.ANY),
    )
    return (
        mean_logits,
        features_grad,
        norm[0, 0],
        bw,
        bm,
        bv,
        bcopy,
        vw,
        vm,
        vv,
        hw[None],
        hm[None],
        hv[None],
        hcopy[None],
        cw,
        cm,
        cv,
    )


def solution(mesh):
    split, whole = P(ALL, None), P()
    heads, biases = P("mem", None, None), P("mem", None)
    return jax.shard_map(
        functools.partial(on_device, mesh),
        mesh=mesh,
        in_specs=(split, P("obj")) + (whole,) * 6 + (heads,) * 3 + (biases,) * 3,
        out_specs=(split, split) + (whole,) * 8 + (heads,) * 4 + (biases,) * 3,
        check_vma=False,
    )
```

```python
import functools
import math

import jax
import jax.numpy as jnp
from jax import lax
from jax.experimental import pallas as pl
from jax.experimental.pallas import tpu as pltpu
from jax.sharding import PartitionSpec as P

STEP = 5
ALL = ("obj", "mem")
LANES = 128
PAD = 16
MIB = 1 << 20

clip_limit = 100.0
beta_one = 0.5
beta_two = 0.5
epsilon = 1e-08
gelu_in = math.sqrt(2.0 / math.pi)
gelu_cube = 0.044715

bf16 = jnp.bfloat16
f32 = jnp.float32
VMEM = pl.BlockSpec(memory_space=pltpu.VMEM)
SMEM = pl.BlockSpec(memory_space=pltpu.SMEM)


def adamw(weight, grad, first, second, rate, decay):
    first_new = beta_one * first + (1.0 - beta_one) * grad
    second_new = beta_two * second + (1.0 - beta_two) * grad * grad
    fix_one = 1.0 / (1.0 - beta_one**STEP)
    fix_two = 1.0 / (1.0 - beta_two**STEP)
    root = lax.rsqrt(second_new * fix_two)
    step_size = first_new * root * (rate * fix_one) / (1.0 + epsilon * root)
    return (weight * (1.0 - rate * decay) - step_size, first_new, second_new)


def dot(a, b, dims=((1,), (0,))):
    return lax.dot_general(a, b, (dims, ((), ())), preferred_element_type=f32)


def call(body, outs, args, scratch=(), name=None, out_spec=VMEM, aliases=None, in_hbm=()):
    specs = [pl.BlockSpec(memory_space=pl.ANY) if i in in_hbm else VMEM for i in range(len(args))]
    return pl.pallas_call(
        body,
        out_shape=outs,
        in_specs=specs,
        out_specs=[out_spec] * len(outs),
        scratch_shapes=list(scratch),
        input_output_aliases=aliases or {},
        compiler_params=pltpu.CompilerParams(vmem_limit_bytes=40 * MIB),
        name=name,
    )(*args)


class Plan:
    def __init__(self, mesh, width, classes, rows):
        self.n_obj, self.n_mem = mesh.shape["obj"], mesh.shape["mem"]
        self.outer = self.n_mem // 2
        self.quads = self.n_obj
        self.shards = 2 * self.quads
        self.width, self.classes, self.rows = width, classes, rows
        self.groups = width // LANES
        self.block_rows = width // self.shards
        self.stacked = self.block_rows * self.groups
        self.items = max(8, self.shards)
        self.bits = [1 << i for i in range(self.outer.bit_length() - 1)]
        self.halving = sorted(range(self.outer), key=lambda k: [k & bit for bit in self.bits])

    def perm(self, move):
        pairs = []
        for obj in range(self.n_obj):
            for mem in range(self.n_mem):
                to_obj, to_mem = move(obj, mem)
                pairs.append((obj * self.n_mem + mem, to_obj * self.n_mem + to_mem))
        return pairs

    def over_core(self, v):
        return lax.ppermute(v, ALL, self.perm(lambda o, m: (o ^ 1, m)))

    def over_plane(self, v, k):
        return lax.ppermute(v, ALL, self.perm(lambda o, m: (o ^ (k >> 1 << 1), m ^ (k & 1))))

    def over_outer(self, v, k):
        return lax.ppermute(v, ALL, self.perm(lambda o, m: (o, m ^ (k << 1))))


def head_body(plan, head_ref, bias_ref, low_ref, held_ref, sem):
    copy = pltpu.make_async_copy(bias_ref, held_ref, sem)
    copy.start()
    low_ref[0 : plan.width, :] = head_ref[...].astype(bf16)
    copy.wait()
    low_ref[plan.width :, :] = jnp.broadcast_to(held_ref[...], (PAD, plan.classes)).astype(bf16)


def low_body(plan, weight_ref, bias_ref, first_ref, second_ref, low_ref, biases_ref):
    low_ref[...] = weight_ref[...].astype(bf16)
    for i, ref in enumerate((bias_ref, first_ref, second_ref)):
        biases_ref[i : i + 1, :] = ref[...]


def forward_body(plan, pieces, *refs):
    feats, (weight_ref, vec_ref) = refs[: len(pieces)], refs[len(pieces) : len(pieces) + 2]
    lifted_ref, mixed_ref, hidden_ref, slope_ref = refs[-4:]
    rows, objs = plan.rows, plan.outer * plan.rows
    outer = place_of()[2]
    tile = 16
    for j in range(2):
        scale_r, scale_s, shift_b = (vec_ref[t, pl.ds(outer * 2 + j, 1), :] for t in range(3))
        first, last = j * objs + pieces[0] * rows, j * objs + (pieces[-1] + 1) * rows
        for k, feat in zip(pieces, feats):
            lifted_ref[j * objs + k * rows : j * objs + (k + 1) * rows, :] = (
                feat[...].astype(f32) * scale_r
            ).astype(bf16)
        mixed_ref[first:last, :] = dot(lifted_ref[first:last, :], weight_ref[...])

        def forward(t, carry):
            at = pl.ds(pl.multiple_of(first + t * tile, tile), tile)
            pre = mixed_ref[at, :] * scale_s + shift_b
            square = pre * pre
            half = 0.5 + 0.5 * jnp.tanh(pre * (gelu_in + (gelu_in * gelu_cube) * square))
            hidden_ref[at, :] = (pre * half).astype(bf16)
            slope_ref[at, :] = half + (half - half * half) * (
                pre * (2.0 * gelu_in + (6.0 * gelu_in * gelu_cube) * square)
            )
            return carry

        steps = (last - first) // tile
        lax.fori_loop(0, steps, forward, 0, unroll=min(steps, 16))


def local_body(plan, *refs):
    n = plan.outer
    feats = refs[:n]
    onehot_ref, weight_ref, vec_ref, own_head, far_head = refs[n : n + 5]
    lifted_ref, mixed_ref, hidden_ref, slope_ref = refs[n + 5 : n + 9]
    send_ref, keep_ref, back_keep, back_send = refs[n + 9 : n + 13]
    dmixed_ref, block_ref, heads_ref, items_ref = refs[n + 13 :]
    rows, width, classes = plan.rows, plan.width, plan.classes
    objs = n * rows
    core, quad, outer, inner = place_of()
    tile = 16

    def member(j):
        return pl.ds(outer * 2 + j, 1)

    items_ref[...] = jnp.zeros_like(items_ref)
    logit_sum = None
    for j in range(2):
        mine = inner == j
        head = jnp.where(mine, own_head[0:width, :], far_head[0:width, :])
        bias = jnp.where(mine, own_head[width : width + 1, :], far_head[width : width + 1, :]).astype(f32)
        hidden = hidden_ref[j * objs : (j + 1) * objs, :]
        logits = dot(hidden, head) + bias
        logit_sum = logits if logit_sum is None else logit_sum + logits
        top = jnp.max(logits, axis=-1, keepdims=True)
        grown = jnp.exp(logits - top)
        soft = grown / jnp.sum(grown, axis=-1, keepdims=True)
        hot = jnp.concatenate(
            [
                onehot_ref[pl.ds(pl.multiple_of(((outer ^ (-p % n)) * 2 + inner) * rows, rows), rows), :]
                for p in range(n)
            ],
            axis=0,
        )
        dlogits = soft - hot
        dlow = dlogits.astype(bf16)
        items_ref[6 + j, 0:1, :] = jnp.sum(dlogits, axis=0, keepdims=True)
        heads_ref[j] = dot(hidden, dlow, ((0,), (0,)))
        mixed_back = dot(dlow, head, ((1,), (1,)))
        block_ref[0:objs, :] = mixed_back
        scale_s = vec_ref[1, member(j), :]

        def backward(t, carry):
            s_sum, b_sum = carry
            at = pl.ds(pl.multiple_of(j * objs + t * tile, tile), tile)
            near = pl.ds(pl.multiple_of(t * tile, tile), tile)
            dpre = block_ref[near, :].astype(bf16).astype(f32) * slope_ref[at, :]
            dmixed_ref[at, :] = (dpre * scale_s).astype(bf16)
            return s_sum + dpre * mixed_ref[at, :], b_sum + dpre

        zero = jnp.zeros((tile, width), f32)
        s_sum, b_sum = lax.fori_loop(0, objs // tile, backward, (zero, zero), unroll=min(objs // tile, 16))
        s_grad = jnp.sum(s_sum, axis=0, keepdims=True)
        b_grad = jnp.sum(b_sum, axis=0, keepdims=True)
        for g in range(plan.groups):
            at = slice(g * LANES, (g + 1) * LANES)
            items_ref[2 + j, g : g + 1, :] = s_grad[:, at]
            items_ref[4 + j, g : g + 1, :] = b_grad[:, at]

    block_ref[...] = dot(dmixed_ref[...], weight_ref[...], ((1,), (1,)))
    r_sums = [jnp.zeros((1, width), f32) for _ in range(2)]
    for spot, k in enumerate(plan.halving):
        p = -k % n
        feat = feats[k][...].astype(f32)
        back = None
        for j in range(2):
            lift_back = block_ref[j * objs + p * rows : j * objs + (p + 1) * rows, :]
            r_sums[j] = r_sums[j] + jnp.sum(lift_back * feat, axis=0, keepdims=True)
            part = lift_back * vec_ref[0, member(j), :]
            back = part if back is None else back + part
        out = back_keep if spot < n // 2 else back_send
        at = slice(spot % (n // 2) * rows, (spot % (n // 2) + 1) * rows)
        out[at, 0:width] = back.astype(out.dtype)
        out[at, width : width + classes] = logit_sum[p * rows : (p + 1) * rows, :].astype(out.dtype)
    for j in range(2):
        for g in range(plan.groups):
            items_ref[j, g : g + 1, :] = r_sums[j][:, g * LANES : (g + 1) * LANES]

    stride = plan.block_rows
    half = width // 2
    for out, side in ((keep_ref, core), (send_ref, 1 - core)):
        part = dot(lifted_ref[:, pl.ds(pl.multiple_of(side * half, half), half)], dmixed_ref[...], ((0,), (0,)))
        for k in range(plan.quads):
            for g in range(plan.groups):
                out[quad ^ k, g * stride : (g + 1) * stride, :] = part[
                    k * stride : (k + 1) * stride, g * LANES : (g + 1) * LANES
                ].astype(out.dtype)
        for k in range(plan.quads):
            shard = side * plan.quads + (quad ^ k)
            at = pl.ds(pl.multiple_of(shard * stride, stride), stride)
            base = plan.stacked
            for j in range(2):
                out[k, base : base + stride, :] = heads_ref[j, at, :].astype(out.dtype)
                base += stride
            out[k, base : base + PAD, :] = items_ref[shard].astype(out.dtype)


def core_body(plan, keep_ref, got_ref, own_ref, *send_refs):
    own_ref[...] = keep_ref[0] + got_ref[0].astype(f32)
    for k in range(1, plan.quads):
        send_refs[-k][...] = (keep_ref[k] + got_ref[k].astype(f32)).astype(bf16)


def place_of():
    obj, mem = lax.axis_index("obj"), lax.axis_index("mem")
    return obj % 2, obj // 2 * 2 + mem % 2, mem // 2, mem % 2


def two_parts(v):
    high = v.astype(bf16).astype(f32)
    return high, v - high


def plane_body(plan, own_ref, *refs):
    got, (send_ref, block_ref, head_ref) = refs[: plan.quads - 1], refs[plan.quads - 1 :]
    total = own_ref[...]
    for r in got:
        total = total + r[...].astype(f32)
    base = plan.stacked
    block_ref[0:base, :] = total[0:base, :]
    send_ref[0:base, :] = total[0:base, :].astype(bf16)
    heads = total[base : base + 2 * plan.block_rows, :]
    head_ref[...] = heads
    squares = jnp.sum(jnp.sum(heads * heads, axis=1, keepdims=True), axis=0, keepdims=True)
    high, low = two_parts(jnp.broadcast_to(squares, (PAD, LANES)))
    items = total[base + 2 * plan.block_rows :, :]
    row = lax.broadcasted_iota(jnp.int32, (PAD, LANES), 0)
    extra = jnp.where(row < plan.groups, items, jnp.where(row == plan.groups, high, low))
    block_ref[base : base + PAD, :] = extra
    send_ref[base : base + PAD, :] = extra.astype(bf16)


def outer_body(plan, block_ref, head_ref, *refs):
    n = plan.outer
    got, (same_ref, flip_ref) = refs[: n - 1], refs[n - 1 :]
    inner = place_of()[3]
    base, stride, groups = plan.stacked, plan.block_rows, plan.groups
    total = block_ref[0:base, :]
    extras = [block_ref[base : base + PAD, :].astype(bf16).astype(f32)]
    for r in got:
        total = total + r[0:base, :].astype(f32)
        extras.append(r[base : base + PAD, :].astype(f32))
    row = lax.broadcasted_iota(jnp.int32, (PAD, LANES), 0)
    head_squares = jnp.zeros((1, LANES), f32)
    item_squares = jnp.zeros((PAD, LANES), f32)
    for extra in extras:
        head_squares = head_squares + extra[groups : groups + 1, :] + extra[groups + 1 : groups + 2, :]
        item_squares = item_squares + jnp.where(row < groups, extra * extra, 0.0)
    squares = (
        jnp.sum(jnp.sum(total * total, axis=1, keepdims=True), axis=0, keepdims=True)
        + jnp.sum(jnp.sum(item_squares, axis=1, keepdims=True), axis=0, keepdims=True)
        + head_squares
    )
    high, low = two_parts(jnp.broadcast_to(squares, (PAD, LANES)))
    items = jnp.concatenate([extra[0:groups, :] for extra in extras], axis=0).astype(bf16)
    sums = jnp.where(row == 0, high, low).astype(bf16)
    block = total.astype(bf16)
    for out, member in ((same_ref, inner), (flip_ref, 1 - inner)):
        at = pl.ds(pl.multiple_of(member * stride, stride), stride)
        out[0:base, :] = block
        out[base : base + groups * n, :] = items
        spot = base + groups * n
        out[spot : spot + stride, :] = head_ref[at, :].astype(bf16)
        out[spot + stride : spot + stride + PAD, :] = sums


def half_body(plan, had_ref, got_ref, keep_ref, send_ref):
    half = keep_ref.shape[0]
    keep_ref[...] = had_ref[0:half, :] + got_ref[0:half, :].astype(f32)
    send_ref[...] = (had_ref[half : 2 * half, :] + got_ref[half : 2 * half, :].astype(f32)).astype(bf16)


def back_body(plan, had_ref, got_ref, feat_ref, mean_ref):
    total = had_ref[...] + got_ref[...].astype(f32)
    feat_ref[...] = total[:, 0 : plan.width]
    mean_ref[...] = total[:, plan.width :] / plan.n_mem


def update_body(plan, *refs):
    chunks = refs[: plan.shards]
    states = refs[plan.shards : plan.shards + 10]
    outs = refs[plan.shards + 10 : plan.shards + 25]
    held, items_ref, sems = refs[plan.shards + 25 : -2], refs[-2], refs[-1]
    bw, bm, bv, vw, vm, vv, hw, hm, hv, cs = states
    norm_out, vec_outs, bias_outs, block_outs, head_outs = (
        outs[0],
        outs[5:8],
        outs[12:15],
        outs[1:5],
        outs[8:12],
    )
    norm_ref, vec_refs, bias_refs, block_refs, head_refs = (
        held[0],
        held[5:8],
        held[12:15],
        held[1:5],
        held[8:12],
    )
    core, quad, outer, inner = place_of()
    n, groups, stride, base = plan.outer, plan.groups, plan.block_rows, plan.stacked
    spot = base + groups * n
    copies = []

    def send(source, target):
        copies.append(pltpu.make_async_copy(source, target, sems.at[len(copies)]))
        copies[-1].start()

    squares = jnp.zeros((1, LANES), f32)
    for chunk in chunks:
        sums = chunk[spot + stride : spot + stride + PAD, :].astype(f32)
        squares = squares + sums[0:1, :] + sums[1:2, :]
    norm = jnp.sqrt(squares)
    norm_ref[...] = norm
    factor = clip_limit / jnp.maximum(norm, clip_limit)
    send(norm_ref, norm_out)

    def shard_of(i):
        side, k = divmod(i, plan.quads)
        return (core ^ side) * plan.quads + (quad ^ k)

    for i, chunk in enumerate(chunks):
        at = pl.ds(pl.multiple_of(shard_of(i) * stride, stride), stride)
        for g in range(groups):
            lanes = slice(g * LANES, (g + 1) * LANES)
            grad = chunk[g * stride : (g + 1) * stride, :].astype(f32) * factor
            new = adamw(bw[at, lanes], grad, bm[at, lanes], bv[at, lanes], 0.02, 0.01)
            for ref, v in zip(block_refs, new + (new[0],)):
                ref[at, lanes] = v.astype(ref.dtype)
        grad = chunk[spot : spot + stride, :].astype(f32) * factor
        new = adamw(hw[at, :], grad, hm[at, :], hv[at, :], 0.02, 0.01)
        for ref, v in zip(head_refs, new + (new[0],)):
            ref[at, :] = v.astype(ref.dtype)
        if i % 2:
            both = pl.ds(pl.multiple_of(shard_of(i) // 2 * (2 * stride), 2 * stride), 2 * stride)
            for source, target in zip(block_refs + head_refs, block_outs + head_outs):
                send(source.at[both], target.at[both])
    for i, chunk in enumerate(chunks):
        shard = shard_of(i)
        items = chunk[base : base + groups * n, :].astype(f32)
        for z in range(n):
            items_ref[shard // 2, (outer ^ z) * 2 + shard % 2] = items[z * groups : (z + 1) * groups, :]
    wide = jnp.concatenate([factor] * groups, axis=1)
    for t in range(3):
        grad = jnp.concatenate([items_ref[t, :, g, :] for g in range(groups)], axis=1) * wide
        for ref, v in zip(vec_refs, adamw(vw[t], grad, vm[t], vv[t], 0.5, 0.0)):
            ref[t] = v
    grad = items_ref[3, outer * 2 + inner, 0:1, :] * factor
    for ref, v in zip(bias_refs, adamw(cs[0:1, :], grad, cs[1:2, :], cs[2:3, :], 0.1, 0.0)):
        ref[...] = v
    for source, target in zip(vec_refs + bias_refs, vec_outs + bias_outs):
        send(source, target)

    for copy in copies:
        copy.wait()


def on_device(
    mesh,
    features,
    labels,
    block_weight,
    block_first,
    block_second,
    member_vectors,
    vectors_first,
    vectors_second,
    head_weight,
    head_first,
    head_second,
    head_bias,
    bias_first,
    bias_second,
):
    rows, width = features.shape
    classes = head_weight.shape[-1]
    plan = Plan(mesh, width, classes, rows)
    n, quads, stride = plan.outer, plan.quads, plan.block_rows
    shape = jax.ShapeDtypeStruct

    far_feats = [plan.over_outer(features, k) for k in range(n - 1, 0, -1)][::-1]
    (own_head,) = call(
        functools.partial(head_body, plan),
        [shape((width + PAD, classes), bf16)],
        [head_weight[0], head_bias],
        [pltpu.VMEM(head_bias.shape, f32), pltpu.SemaphoreType.DMA],
        name="head_low",
        in_hbm=(1,),
    )
    far_head = plan.over_plane(own_head, 1)
    weight_low, biases = call(
        functools.partial(low_body, plan),
        [shape((width, width), bf16), shape((3, classes), f32)],
        [block_weight, head_bias, bias_first, bias_second],
        name="weight_low",
    )
    onehot = (
        jnp.arange(classes, dtype=jnp.int32)[None, :] == labels[:, None]
    ).astype(f32)

    objs = n * rows
    total = plan.stacked + 2 * stride + PAD
    back = width + classes
    done = ()
    for pieces in (range(n),):
        done = call(
            functools.partial(forward_body, plan, pieces),
            [shape((2 * objs, width), dtype) for dtype in (bf16, f32, bf16, f32)],
            [([features] + far_feats)[-k] for k in pieces] + [weight_low, member_vectors, *done],
            name="forward",
            aliases={3 + i: i for i in range(len(done))},
        )
    outs = call(
        functools.partial(local_body, plan),
        [
            shape((quads, total, LANES), bf16),
            shape((quads, total, LANES), f32),
            shape((objs // 2, back), f32),
            shape((objs // 2, back), bf16),
        ],
        [features, *far_feats, onehot, weight_low, member_vectors, own_head, far_head, *done],
        [
            pltpu.VMEM((2 * objs, width), bf16),
            pltpu.VMEM((2 * objs, width), f32),
            pltpu.VMEM((2, width, classes), f32),
            pltpu.VMEM((plan.items, PAD, LANES), f32),
        ],
        name="local",
    )
    send, keep, back_keep, back_send = outs

    got = plan.over_core(send)
    own, *sends = call(
        functools.partial(core_body, plan),
        [shape((total, LANES), f32)] + [shape((total, LANES), bf16)] * (quads - 1),
        [keep, got],
        name="core_sum",
    )
    got = [plan.over_plane(v, quads - 1 - k) for k, v in enumerate(sends)]
    for bit in plan.bits[:-1]:
        half = back_keep.shape[0] // 2
        back_keep, back_send = call(
            functools.partial(half_body, plan),
            [shape((half, back), f32), shape((half, back), bf16)],
            [back_keep, plan.over_outer(back_send, bit)],
            name="back_half",
        )
    own, back_send, back_keep = lax.optimization_barrier((own, back_send, back_keep))
    send, block, heads = call(
        functools.partial(plane_body, plan),
        [
            shape((plan.stacked + PAD, LANES), bf16),
            shape((plan.stacked + PAD, LANES), f32),
            shape((2 * stride, LANES), f32),
        ],
        [own, *got],
        name="plane_sum",
    )
    got = [plan.over_outer(send, k) for k in range(1, n)]
    features_grad, mean_logits = call(
        functools.partial(back_body, plan),
        [shape((rows, width), f32), shape((rows, classes), f32)],
        [back_keep, plan.over_outer(back_send, plan.bits[-1])],
        name="back_sum",
    )
    got, features_grad, mean_logits = lax.optimization_barrier((got, features_grad, mean_logits))
    last = plan.stacked + plan.groups * n + stride + PAD
    same, flip = call(
        functools.partial(outer_body, plan),
        [shape((last, LANES), bf16)] * 2,
        [block, heads, *got],
        name="outer_sum",
    )
    near = [same] + [plan.over_plane(flip if k & 1 else same, k) for k in range(1, quads)]
    far = [plan.over_core(v) for v in near]

    like = lambda v, dtype=f32: (v.shape, dtype)
    head_w, head_m, head_v = head_weight[0], head_first[0], head_second[0]
    results = (
        [((1, LANES), f32)]
        + [like(block_weight)] * 3
        + [like(block_weight, bf16)]
        + [like(member_vectors)] * 3
        + [like(head_w)] * 3
        + [like(head_w, bf16)]
        + [like(head_bias)] * 3
    )
    (norm, bw, bm, bv, bcopy, vw, vm, vv, hw, hm, hv, hcopy, cw, cm, cv) = call(
        functools.partial(update_body, plan),
        [shape(*r) for r in results],
        [
            *near,
            *far,
            block_weight,
            block_first,
            block_second,
            member_vectors,
            vectors_first,
            vectors_second,
            head_w,
            head_m,
            head_v,
            biases,
        ],
        [pltpu.VMEM(*r) for r in results]
        + [
            pltpu.VMEM((plan.items // 2, plan.n_mem, plan.groups, LANES), f32),
            pltpu.SemaphoreType.DMA((7 + 8 * plan.quads,)),
        ],
        name="update",
        out_spec=pl.BlockSpec(memory_space=pl.ANY),
    )
    return (
        mean_logits,
        features_grad,
        norm[0, 0],
        bw,
        bm,
        bv,
        bcopy,
        vw,
        vm,
        vv,
        hw[None],
        hm[None],
        hv[None],
        hcopy[None],
        cw,
        cm,
        cv,
    )


def solution(mesh):
    split, whole = P(ALL, None), P()
    heads, biases = P("mem", None, None), P("mem", None)
    return jax.shard_map(
        functools.partial(on_device, mesh),
        mesh=mesh,
        in_specs=(split, P("obj")) + (whole,) * 6 + (heads,) * 3 + (biases,) * 3,
        out_specs=(split, split) + (whole,) * 8 + (heads,) * 4 + (biases,) * 3,
        check_vma=False,
    )
```
